256 devices in a mesh: sec: 2 (over y_hi), dp: 16 (over x, y_lo, core), tp: 8 (over z).
Axes of the slice: x: 4, y: 4 (y_hi: 2, y_lo: 2; y = y_hi * 2 + y_lo), z: 8, core: 2. Of those that a mesh axis runs over, the one named last changes fastest.
Arguments:
- latents: bfloat16 [256, 64, 1280], P(('dp', 'tp')), may hold values from -6 to 6
- timesteps: int32 [256], P(('dp', 'tp')), may hold values from 0 to 24
- prompt_ids: int32 [256], P(('dp', 'tp')), may hold values from 0 to 63
- prompt_table: bfloat16 [64, 1280], replicated, may hold values from -6 to 6
- gains: float32 [2, 1280], replicated, may hold values from 0.5 to 1.5
- w_in: bfloat16 [2, 1280, 5120], P('sec', None, 'tp'), may hold values from -0.15625 to 0.15625
- w_out: bfloat16 [2, 1280, 5120], P('sec', None, 'tp'), may hold values from -0.078125 to 0.078125
Outputs:
- grad_in: float32 [1280, 5120], P(('sec', 'dp'), 'tp')
- grad_out: float32 [1280, 5120], P(('sec', 'dp'), 'tp')
The draws below stay inside these ranges and needn't reach their ends.
All inputs are finite; a program needn't handle non-finite values.
Results may differ from the reference program's by a relative error of at most 0.03.
Values may be sent and summed in bfloat16 or wider, within the bound.
A program may use at most 64 MiB of HBM per device.

```python
import math
import jax
import jax.numpy as jnp
from jax import lax

D = 1280
H = 5120
TOK = 64
STEPS = 50
PROMPTS = 64
IMAGES = 256
N_TP = 8


def touch_ends(drawn, stream_key, smallest, largest):
    shape = drawn.shape
    index_at = [jax.random.randint(jax.random.fold_in(stream_key, axis), (), 0, shape[axis]) for axis in range(len(shape))]
    drawn = drawn.at[tuple(index_at)].set(smallest)
    longest = shape.index(max(shape))
    index_at[longest] = (index_at[longest] + 1) % shape[longest]
    return drawn.at[tuple(index_at)].set(largest)


def levels(rng, shape, pieces, low, largest):
    loudness, own = 1.0, jax.random.fold_in(rng, 6)
    for position, shards_of in pieces:
        heights = jnp.exp(jax.random.uniform(jax.random.fold_in(own, position), (shards_of,), jnp.float32, low / len(pieces), largest / len(pieces)))
        loudness = loudness * jnp.repeat(heights, shape[position] // shards_of).reshape([-1 if axis == position else 1 for axis in range(len(shape))])
    return loudness


def bell_draw(own_key, extent, width, bound, cuts=(), kind=jnp.bfloat16):
    factor_of = levels(own_key, extent, cuts, -0.22, 0.18) if cuts else 1.0
    entries = jax.random.normal(own_key, extent, jnp.float32) * width * factor_of
    return jnp.minimum(jnp.maximum(entries, -bound), bound).astype(kind)


def setup_inputs(seed: int = 0) -> dict:
    key_of = jax.random.split(jax.random.key(seed), 8)
    latents = bell_draw(key_of[0], (IMAGES, TOK, D), 1.0, 6.0, ((0, 128),))
    timesteps = touch_ends(jax.random.randint(key_of[1], (IMAGES,), 0, STEPS // 2), jax.random.fold_in(key_of[1], 1), 0, (STEPS // 2) - 1).astype(jnp.int32)
    prompt_ids = touch_ends(jax.random.randint(key_of[2], (IMAGES,), 0, PROMPTS), jax.random.fold_in(key_of[2], 1), 0, PROMPTS - 1).astype(jnp.int32)
    prompt_table = bell_draw(key_of[3], (PROMPTS, D), 1.0, 6.0)
    gains = jnp.clip(1.0 + 0.1 * jax.random.normal(key_of[4], (2, D), jnp.float32), 0.5, 1.5)
    w_in = bell_draw(key_of[5], (2, D, H), D ** -0.5, 0.15625, ((0, 2), (2, 8)))
    w_out = bell_draw(key_of[6], (2, D, H), H ** -0.5, 0.078125, ((0, 2), (2, 8)))
    return {"latents": latents, "timesteps": timesteps, "prompt_ids": prompt_ids, "prompt_table": prompt_table, "gains": gains, "w_in": w_in, "w_out": w_out}


EPS = 1e-06

def gelu_slope(value):
    return 0.5 * (1.0 + lax.erf(value / math.sqrt(2.0))) + value * jnp.exp(-0.5 * value * value) / math.sqrt(2.0 * math.pi)

def normed(rows, gain):
    scale = lax.rsqrt(lax.optimization_barrier(jnp.mean(rows * rows, axis=-1, keepdims=True)) + EPS)
    return ((rows * scale * gain).astype(jnp.bfloat16), scale)

def blocked_sum(left, right):
    share = left.shape[1] // N_TP
    total = jnp.zeros((left.shape[0], right.shape[0]), jnp.float32)
    for part in range(N_TP):
        piece = lax.dot_general(left[:, part * share:(part + 1) * share], right[:, part * share:(part + 1) * share], (((1,), (1,)), ((), ())), preferred_element_type=jnp.float32)
        rounded = lax.optimization_barrier(piece.astype(jnp.bfloat16))
        total = total + rounded.astype(jnp.float32)
    return total

def forward(rows, gain, weight_in, weight_out):
    base = rows.astype(jnp.float32)
    xn, scale = normed(base, gain)
    hp = jnp.dot(xn, weight_in, preferred_element_type=jnp.float32)
    act = jax.nn.gelu(hp, approximate=False).astype(jnp.bfloat16)
    return (base + blocked_sum(act, weight_out), xn, hp, act, scale)

def score_of(pooled, text):
    unit_img = pooled * lax.rsqrt(lax.optimization_barrier(jnp.mean(pooled * pooled, axis=-1, keepdims=True)) + EPS)
    unit_txt = text * lax.rsqrt(lax.optimization_barrier(jnp.mean(text * text, axis=-1, keepdims=True)) + EPS)
    return 100.0 * lax.optimization_barrier(jnp.sum(unit_img * unit_txt, axis=-1)) / pooled.shape[-1]

def reference(latents, timesteps, prompt_ids, prompt_table, gains, w_in, w_out):
    rows = latents.reshape(IMAGES * TOK, D)
    theta = math.pi / 2.0 * (timesteps.astype(jnp.float32) + 1.0) / (STEPS + 1.0)
    alpha = jnp.repeat(jnp.cos(theta), TOK)[:, None]
    sigma = jnp.repeat(jnp.sin(theta), TOK)[:, None]
    eps, xn0, hp0, act0, unused = forward(rows, gains[0], w_in[0], w_out[0])
    images = ((rows.astype(jnp.float32) - sigma * eps) / alpha).astype(jnp.bfloat16)
    seen, xn1, hp1, act1, scale1 = forward(images, gains[1], w_in[1], w_out[1])
    pooled = lax.optimization_barrier(jnp.mean(seen.reshape(IMAGES, TOK, D), axis=1))
    text = prompt_table[prompt_ids].astype(jnp.float32)
    g_pooled = jax.grad(lambda p: -jnp.sum(score_of(p, text)))(pooled)
    g_mean = g_pooled / TOK
    g_tok = g_mean.astype(jnp.bfloat16)
    g_h1 = jnp.dot(g_tok, w_out[1], preferred_element_type=jnp.float32)
    g_hp1 = (jnp.repeat(g_h1, TOK, axis=0) * gelu_slope(hp1)).astype(jnp.bfloat16)
    g_xn1 = blocked_sum(g_hp1, w_in[1])
    base1 = images.astype(jnp.float32)
    weighted = gains[1] * g_xn1
    g_norm = scale1 * weighted - base1 * scale1 ** 3 * lax.optimization_barrier(jnp.mean(base1 * weighted, axis=-1, keepdims=True))
    g_images = (jnp.repeat(g_mean, TOK, axis=0) + g_norm).astype(jnp.bfloat16)
    g_eps = (-(sigma / alpha) * g_images.astype(jnp.float32)).astype(jnp.bfloat16)
    grad_out = lax.dot_general(g_eps, act0, (((0,), (0,)), ((), ())), preferred_element_type=jnp.float32)
    g_hp0 = (jnp.dot(g_eps, w_out[0], preferred_element_type=jnp.float32) * gelu_slope(hp0)).astype(jnp.bfloat16)
    grad_in = lax.dot_general(xn0, g_hp0, (((0,), (0,)), ((), ())), preferred_element_type=jnp.float32)
    return (grad_in, grad_out)
```

```python
import math

import jax
import jax.numpy as jnp
from jax import lax
from jax.sharding import PartitionSpec as P

STEPS = 50
EPS = 1e-06


def gelu_slope(value):
    return 0.5 * (1.0 + lax.erf(value / math.sqrt(2.0))) + value * jnp.exp(
        -0.5 * value * value
    ) / math.sqrt(2.0 * math.pi)


def normed(rows, gain):
    scale = lax.rsqrt(jnp.mean(rows * rows, axis=-1, keepdims=True) + EPS)
    return ((rows * scale * gain).astype(jnp.bfloat16), scale)


def score_of(pooled, text):
    unit_img = pooled * lax.rsqrt(jnp.mean(pooled * pooled, axis=-1, keepdims=True) + EPS)
    unit_txt = text * lax.rsqrt(jnp.mean(text * text, axis=-1, keepdims=True) + EPS)
    return 100.0 * jnp.sum(unit_img * unit_txt, axis=-1) / pooled.shape[-1]


def collect(piece):
    return lax.all_gather(piece, "tp", axis=0, tiled=True)


def reduce_rows(value):
    return lax.psum_scatter(value, "tp", scatter_dimension=0, tiled=True).astype(jnp.float32)


def contract_last(left, right):
    return lax.dot_general(left, right, (((1,), (1,)), ((), ())), preferred_element_type=jnp.float32)


def contract_first(left, right):
    return lax.dot_general(left, right, (((0,), (0,)), ((), ())), preferred_element_type=jnp.float32)


def on_device(latents, timesteps, prompt_ids, prompt_table, gains, w_in, w_out):
    count, tokens, width = latents.shape
    segment = lax.axis_index("sec")
    swap = [(0, 1), (1, 0)]
    other_in = lax.ppermute(w_in[0], "sec", swap)
    other_out = lax.ppermute(w_out[0], "sec", swap)
    first = segment == 0
    win0 = jnp.where(first, w_in[0], other_in)
    wout0 = jnp.where(first, w_out[0], other_out)
    win1 = jnp.where(first, other_in, w_in[0])
    wout1 = jnp.where(first, other_out, w_out[0])
    own = lax.dynamic_index_in_dim(latents, segment, 0, keepdims=False)
    step = lax.dynamic_index_in_dim(timesteps, segment, 0, keepdims=False)
    prompt = lax.dynamic_index_in_dim(prompt_ids, segment, 0, keepdims=True)
    theta = math.pi / 2.0 * (step.astype(jnp.float32) + 1.0) / (STEPS + 1.0)
    alpha, sigma = jnp.cos(theta), jnp.sin(theta)

    xn0, _ = normed(collect(own).astype(jnp.float32), gains[0])
    hp0 = jnp.dot(xn0, win0, preferred_element_type=jnp.float32)
    act0 = jax.nn.gelu(hp0, approximate=False).astype(jnp.bfloat16)
    mix0 = reduce_rows(contract_last(act0, wout0).astype(jnp.bfloat16))
    base = own.astype(jnp.float32)
    images = ((base - sigma * (base + mix0)) / alpha).astype(jnp.bfloat16)

    seen = images.astype(jnp.float32)
    xn1, _ = normed(collect(images).astype(jnp.float32), gains[1])
    hp1 = jnp.dot(xn1, win1, preferred_element_type=jnp.float32)
    act1 = jax.nn.gelu(hp1, approximate=False).astype(jnp.bfloat16).astype(jnp.float32)
    mean1 = jnp.mean(act1.reshape(-1, tokens, act1.shape[-1]), axis=1)
    high = mean1.astype(jnp.bfloat16)
    low = (mean1 - high.astype(jnp.float32)).astype(jnp.bfloat16)
    mix1 = reduce_rows(contract_last(high, wout1) + contract_last(low, wout1))
    pooled = jnp.mean(seen, axis=0, keepdims=True) + mix1
    onehot = (prompt[:, None] == jnp.arange(prompt_table.shape[0], dtype=jnp.int32)[None, :]).astype(
        jnp.bfloat16
    )
    text = jnp.dot(onehot, prompt_table, preferred_element_type=jnp.float32)
    g_mean = jax.grad(lambda p: -jnp.sum(score_of(p, text)))(pooled) / tokens
    all_tok = collect(g_mean.astype(jnp.bfloat16))
    g_h1 = jnp.dot(all_tok, wout1, preferred_element_type=jnp.float32)
    slope1 = gelu_slope(hp1).reshape(-1, tokens, hp1.shape[-1])
    g_hp1 = (g_h1[:, None, :] * slope1).reshape(hp1.shape).astype(jnp.bfloat16)
    g_xn = reduce_rows(contract_last(g_hp1, win1).astype(jnp.bfloat16))
    scale1 = lax.rsqrt(jnp.mean(seen * seen, axis=-1, keepdims=True) + EPS)
    weighted = gains[1] * g_xn
    g_norm = scale1 * weighted - seen * scale1**3 * jnp.mean(seen * weighted, axis=-1, keepdims=True)
    g_images = (g_mean + g_norm).astype(jnp.bfloat16)
    g_eps = (-(sigma / alpha) * g_images.astype(jnp.float32)).astype(jnp.bfloat16)

    g_all = collect(g_eps)
    grad_w_out = contract_first(g_all, act0)
    g_hp0 = (jnp.dot(g_all, wout0, preferred_element_type=jnp.float32) * gelu_slope(hp0)).astype(
        jnp.bfloat16
    )
    grad_w_in = contract_first(xn0, g_hp0)
    return tuple(
        lax.psum_scatter(
            value.astype(jnp.bfloat16), ("sec", "dp"), scatter_dimension=0, tiled=True
        ).astype(jnp.float32)
        for value in (grad_w_in, grad_w_out)
    )


def solution(mesh):
    in_specs = (
        P(("dp", "tp"), None, None),
        P(("dp", "tp")),
        P(("dp", "tp")),
        P(),
        P(),
        P("sec", None, "tp"),
        P("sec", None, "tp"),
    )
    out_specs = (P(("sec", "dp"), "tp"), P(("sec", "dp"), "tp"))
    return jax.shard_map(
        on_device, mesh=mesh, in_specs=in_specs, out_specs=out_specs, check_vma=False
    )
```

```python
import functools
import math

import jax
import jax.numpy as jnp
from jax import lax
from jax.experimental import pallas as pl
from jax.experimental.pallas import tpu as pltpu
from jax.sharding import PartitionSpec as P

STEPS = 50
EPS = 1e-06
MESH = pl.DeviceIdType.MESH
F32, BF16 = jnp.float32, jnp.bfloat16

ORDER = (4, 5, 3, 6, 2, 7, 1, 0)
POS = {slot: pos for pos, slot in enumerate(ORDER)}
NZ, NR = 8, 4


def gelu_and_slope(value):
    cdf = 0.5 * (1.0 + lax.erf(value * (1.0 / math.sqrt(2.0))))
    pdf = jnp.exp(-0.5 * value * value) * (1.0 / math.sqrt(2.0 * math.pi))
    return value * cdf, cdf + value * pdf


def nt(left, right):
    return lax.dot_general(left, right, (((1,), (1,)), ((), ())), preferred_element_type=F32)


def tn(left, right):
    return lax.dot_general(left, right, (((0,), (0,)), ((), ())), preferred_element_type=F32)


def kernel(
    lat, steps, ids, table, gains, win, wout, gin, gout,
    w_in, w_out, lats, xn0, h0, sl0, imgs, xn1, sl1, gh1, geps, gh0, hp, pf, pf2, stg1, rcv1, stg2,
    rcv2, idb, hm, pm, pmsg, prcv, acc, cstg, crcv, rstg, rrcv, tstg, tsum, trcv,
    local_sem, w_send, w_recv, ag_send, ag_recv, rs_send, rs_recv, id_send, id_recv, p_send, p_recv,
    c_send, c_recv, g_send, g_recv, t_send, t_recv,
):
    tok, width = lat.shape[1], lat.shape[2]
    half = tok // 2
    hidden = win.shape[2]
    sec, dp, me = lax.axis_index("sec"), lax.axis_index("dp"), lax.axis_index("tp")
    x, ylo, core = dp // 4, (dp // 2) % 2, dp % 2
    y = sec * 2 + ylo
    other = 1 - sec

    def at_z(distance):
        return {"tp": (me + distance + NZ) % NZ}

    def at_x(distance):
        return {"dp": ((x + distance + NR) % NR) * 4 + ylo * 2 + core}

    def at_y(distance):
        there = (y + distance + NR) % NR
        return {"sec": there // 2, "dp": x * 4 + (there % 2) * 2 + core}

    partner = {"dp": x * 4 + ylo * 2 + (1 - core)}
    across = {"sec": other, "dp": x * 4 + (1 - ylo) * 2 + core}
    pending = []

    def remote(src, dst, send_sem, recv_sem, device):
        return pltpu.make_async_remote_copy(
            src_ref=src, dst_ref=dst, send_sem=send_sem, recv_sem=recv_sem,
            device_id=device, device_id_type=MESH,
        )

    def go(copy):
        copy.start()
        pending.append(copy)

    here = [
        pltpu.make_async_copy(lat.at[sec], lats.at[pl.ds(POS[0] * tok, tok)], local_sem.at[0]),
        pltpu.make_async_copy(win.at[0], w_in.at[sec], local_sem.at[1]),
        pltpu.make_async_copy(wout.at[0], w_out.at[sec], local_sem.at[2]),
    ]
    for copy in here:
        copy.start()
    idb[0] = jnp.full((8, 128), ids[sec], jnp.int32)

    peers = [at_z(k) for k in range(1, NZ)] + [partner]
    peers += [at_x(k) for k in range(1, NR)] + [at_y(k) for k in range(1, NR)]
    barrier = pltpu.get_barrier_semaphore()
    for peer in peers:
        pl.semaphore_signal(barrier, inc=1, device_id=peer, device_id_type=MESH)
    pl.semaphore_wait(barrier, len(peers))

    def gather_copy(phase, buf, way, step, part):
        if way == 0:
            src, dst, device = POS[step - 1], POS[step], at_z(1)
        else:
            src, dst, device = POS[(NZ - step + 1) % NZ], POS[NZ - step], at_z(-1)
        at = (phase, way, 2 * (step - 1) + part)
        return remote(
            buf.at[pl.ds(src * tok + part * half, half)],
            buf.at[pl.ds(dst * tok + part * half, half)],
            ag_send.at[at], ag_recv.at[at], device,
        )

    def gather_begin(phase, buf, part):
        for way in (0, 1):
            go(gather_copy(phase, buf, way, 1, part))

    def gather_step(phase, buf, step):
        for part in (0, 1):
            for way in (0, 1):
                if step == NZ // 2 and part != way:
                    continue
                gather_copy(phase, buf, way, step, part).wait_recv()
                if step + 1 < NZ // 2 or (step + 1 == NZ // 2 and part == way):
                    go(gather_copy(phase, buf, way, step + 1, part))

    def arrived(step):
        if step == 0:
            return POS[0] * tok, tok
        if step == NZ // 2:
            return 0, tok
        return POS[NZ - step] * tok, 2 * tok

    def scatter_copy(phase, stg, rcv, way, step, part):
        at = (phase, way, 2 * (step - 1) + part)
        rows = pl.ds(part * half, half)
        return remote(
            stg.at[way, step - 1, rows], rcv.at[way, step - 1, rows],
            rs_send.at[at], rs_recv.at[at], at_z(1) if way == 0 else at_z(-1),
        )

    def scatter_step(phase, stg, rcv, step):
        rows = [(part, way) for part in (0, 1) for way in (0, 1)]
        if step == 1:
            rows = [(0, 0), (1, 1)]
        if step == 2:
            rows = [(1, 0), (0, 1), (0, 0), (1, 1)]
        for part, way in rows:
            at = pl.ds(part * half, half)
            base = part * half + (way * tok if step > 1 else 0)
            value = pf[pl.ds(base, half), :]
            if step > 2 or (step == 2 and part == way):
                scatter_copy(phase, stg, rcv, way, step - 1, part).wait_recv()
                value = value + rcv[way, step - 2, at, :].astype(F32)
            stg[way, step - 1, at, :] = value.astype(BF16)
            go(scatter_copy(phase, stg, rcv, way, step, part))

    def scatter_end(phase, stg, rcv, part):
        for way in (0, 1):
            scatter_copy(phase, stg, rcv, way, NZ // 2, part).wait_recv()

    def chunk(step):
        return arrived(5 - step) if step > 1 else (0, tok)

    def piece(quarter):
        return pl.ds(pl.multiple_of((quarter % 4) * 320 + core * 160, 32), 160)

    held = (w_in, w_out)
    given = (win, wout)

    def weight_copy(a, kind):
        if kind < 2:
            rows = piece(x + 2 * kind)
            src, dst, device = given[a].at[0, rows], held[a].at[sec, rows], across
        elif kind < 4:
            rows = piece(x)
            src = dst = held[a].at[other, rows]
            device = at_x(1) if kind == 2 else at_x(-1)
        else:
            rows = piece(x + (0, 2, 3, 1)[kind - 4])
            src = dst = held[a].at[other, rows]
            device = partner
        return remote(src, dst, w_send.at[a, kind], w_recv.at[a, kind], device)

    def weight_landed(a, kind):
        if kind < 4:
            rows = piece(x + (0, 2, 3, 1)[kind])
        else:
            quarter = (x + (0, 2, 3, 1)[kind - 4]) % 4
            rows = pl.ds(pl.multiple_of(quarter * 320 + (1 - core) * 160, 32), 160)
        ref = held[a].at[other, rows]
        remote(ref, ref, w_send.at[a, kind], w_recv.at[a, kind], partner).wait_recv()

    def weights_first(a):
        weight_landed(a, 0)
        go(weight_copy(a, 2))
        go(weight_copy(a, 3))
        go(weight_copy(a, 4))
        go(weight_copy(a, 1))

    def weights_second(a):
        for kind in (2, 3, 1):
            weight_landed(a, kind)
            go(weight_copy(a, {2: 6, 3: 7, 1: 5}[kind]))

    def weights_last(a):
        for kind in (4, 6, 7, 5):
            weight_landed(a, kind)

    def each(count, rows, body, init=None):
        return lax.fori_loop(0, count // rows, lambda i, c: body(pl.multiple_of(i * rows, rows), c), init)

    def norm(buf, dst, start, count, gain, slots=None):
        def body(at, total):
            value = buf[pl.ds(start + at, 16), :].astype(F32)
            scale = lax.rsqrt(jnp.mean(value * value, axis=-1, keepdims=True) + EPS)
            dst[pl.ds(start + at, 16), :] = (value * scale * gain).astype(BF16)
            return None if total is None else total + value[:8] + value[8:]

        if slots is None:
            each(count, 16, body)
            return
        for index, slot in enumerate(slots):
            start = POS[slot] * tok
            total = each(tok, 16, body, jnp.zeros((8, width), F32))
            pm[pl.ds(slot, 1), :] = jnp.sum(total, axis=0, keepdims=True) * (1.0 / tok)

    def slots_of(start, count):
        return ORDER[start // tok:(start + count) // tok]

    theta = (jnp.full((1, 128), steps[sec], jnp.int32).astype(F32) + 1.0) * (
        math.pi / 2.0 / (STEPS + 1.0)
    )
    alpha, sigma = jnp.cos(theta)[:, :1], jnp.sin(theta)[:, :1]
    go(weight_copy(0, 0))
    here[0].wait()
    for part in (0, 1):
        gather_begin(0, lats, part)
    for k in range(1, NZ):
        go(remote(idb.at[0], idb.at[k], id_send.at[k - 1], id_recv.at[k - 1], at_z(k)))
    gain0, gain1 = gains[0:1, :], gains[1:2, :]
    norm(lats, xn0, *arrived(0), gain0)
    gather_step(0, lats, 1)
    weights_first(0)
    norm(lats, xn0, *arrived(1), gain0)
    gather_step(0, lats, 2)
    weights_second(0)
    go(weight_copy(1, 0))
    norm(lats, xn0, *arrived(2), gain0)
    gather_step(0, lats, 3)
    norm(lats, xn0, *arrived(3), gain0)
    gather_step(0, lats, 4)
    norm(lats, xn0, *arrived(4), gain0)
    weights_last(0)
    weights_first(1)
    here[1].wait()

    def hidden0(start, count):
        hp[pl.ds(0, count), :] = jnp.dot(
            xn0[pl.ds(start, count), :], w_in[0], preferred_element_type=F32
        )

        def body(at, carry):
            act, slope = gelu_and_slope(hp[pl.ds(at, 16), :])
            h0[pl.ds(start + at, 16), :] = act.astype(BF16)
            sl0[pl.ds(start + at, 16), :] = slope
            return carry

        each(count, 16, body)

    for step in range(1, 6):
        hidden0(*chunk(step))
        if step == 1:
            weights_second(1)
    weights_last(1)
    here[2].wait()

    for step in range(1, 6):
        start, count = chunk(step)
        out = nt(h0[pl.ds(start, count), :], w_out[0])
        if step < 5:
            pf[pl.ds(0, count), :] = out
            scatter_step(0, stg1, rcv1, step)
        else:
            pf2[...] = out

    own = POS[0] * tok
    for part in (0, 1):
        scatter_end(0, stg1, rcv1, part)

        def images(at, carry):
            rows = pl.ds(part * half + at, 16)
            base = lats[pl.ds(own + part * half + at, 16), :].astype(F32)
            mix = pf2[rows, :] + (rcv1[0, 3, rows, :].astype(F32) + rcv1[1, 3, rows, :].astype(F32))
            imgs[pl.ds(own + part * half + at, 16), :] = (
                (base - sigma * (base + mix)) / alpha
            ).astype(BF16)
            return carry

        each(half, 16, images)
        gather_begin(1, imgs, part)

    def hidden1(start, count):
        slots = slots_of(start, count)
        norm(imgs, xn1, start, count, gain1, slots)
        hp[pl.ds(0, count), :] = jnp.dot(
            xn1[pl.ds(start, count), :], w_in[1], preferred_element_type=F32
        )
        for index, slot in enumerate(slots):
            def body(at, total):
                act, slope = gelu_and_slope(hp[pl.ds(index * tok + at, 16), :])
                sl1[pl.ds(start + index * tok + at, 16), :] = slope
                act = act.astype(BF16).astype(F32)
                return total + act[:8] + act[8:]

            total = each(tok, 16, body, jnp.zeros((8, hidden), F32))
            hm[pl.ds(slot, 1), :] = jnp.sum(total, axis=0, keepdims=True) * (1.0 / tok)

    hidden1(*arrived(0))
    for k in range(1, NZ):
        remote(idb.at[k], idb.at[k], id_send.at[k - 1], id_recv.at[k - 1], at_z(k)).wait_recv()
    id_rows = jnp.concatenate([idb[k, 0:1, :] for k in range(NZ)], axis=0)
    prompts = table.shape[0]
    onehot = (
        id_rows[:, :prompts] == lax.broadcasted_iota(jnp.int32, (NZ, prompts), 1)
    ).astype(F32).astype(BF16)
    text = jnp.dot(onehot, table[...], preferred_element_type=F32)
    text = text * lax.rsqrt(jnp.mean(text * text, axis=-1, keepdims=True) + EPS)
    for step in range(1, 5):
        gather_step(1, imgs, step)
        hidden1(*arrived(step))

    mean1 = hm[...]
    high = mean1.astype(BF16).astype(F32)
    both = jnp.concatenate([high, mean1 - high], axis=0).astype(BF16)
    mixed = nt(both, w_out[1])
    mixed = mixed[:NZ] + mixed[NZ:]
    mid = width // 2
    pmsg[...] = jnp.concatenate([mixed[:, :mid], mixed[:, mid:]], axis=0).astype(BF16)
    for k in range(1, NZ):
        go(remote(pmsg, prcv.at[k - 1], p_send.at[k - 1], p_recv.at[k - 1], at_z(k)))
    pooled = pm[...] + mixed
    for k in range(1, NZ):
        remote(pmsg, prcv.at[k - 1], p_send.at[k - 1], p_recv.at[k - 1], at_z(k)).wait_recv()
        got = prcv[k - 1].astype(F32)
        got = jnp.concatenate([got[:NZ], got[NZ:]], axis=1)
        pooled = pooled + jnp.concatenate([got[NZ - k:], got[:NZ - k]], axis=0)
    unit = lax.rsqrt(jnp.mean(pooled * pooled, axis=-1, keepdims=True) + EPS)
    g_mean = (unit * text - pooled * (unit * unit * unit) * jnp.mean(
        pooled * text, axis=-1, keepdims=True
    )) * (-100.0 / width / tok)
    g_h1 = jnp.dot(g_mean.astype(BF16), w_out[1], preferred_element_type=F32)
    g_own = g_mean[0:1, :]

    for step in range(1, 6):
        start, count = chunk(step)
        for index, slot in enumerate(slots_of(start, count)):
            row = g_h1[slot:slot + 1, :]

            def slope_times(at, carry):
                rows = pl.ds(start + index * tok + at, 16)
                gh1[rows, :] = (row * sl1[rows, :]).astype(BF16)
                return carry

            each(tok, 16, slope_times)
        out = nt(gh1[pl.ds(start, count), :], w_in[1])
        if step < 5:
            pf[pl.ds(0, count), :] = out
            scatter_step(1, stg2, rcv2, step)
        else:
            pf2[...] = out

    ratio = -(sigma / alpha)
    for part in (0, 1):
        scatter_end(1, stg2, rcv2, part)

        def back(at, carry):
            rows = pl.ds(part * half + at, 16)
            seen = imgs[pl.ds(own + part * half + at, 16), :].astype(F32)
            g_xn = pf2[rows, :] + (
                rcv2[0, 3, rows, :].astype(F32) + rcv2[1, 3, rows, :].astype(F32)
            )
            scale = lax.rsqrt(jnp.mean(seen * seen, axis=-1, keepdims=True) + EPS)
            weighted = gain1 * g_xn
            g_norm = scale * weighted - seen * (scale * scale * scale) * jnp.mean(
                seen * weighted, axis=-1, keepdims=True
            )
            g_images = (g_own + g_norm).astype(BF16).astype(F32)
            geps[pl.ds(own + part * half + at, 16), :] = (ratio * g_images).astype(BF16)
            return carry

        each(half, 16, back)
        gather_begin(2, geps, part)

    def hidden_back(start, count):
        hp[pl.ds(0, count), :] = jnp.dot(
            geps[pl.ds(start, count), :], w_out[0], preferred_element_type=F32
        )

        def body(at, carry):
            rows = pl.ds(start + at, 16)
            gh0[rows, :] = (hp[pl.ds(at, 16), :] * sl0[rows, :]).astype(BF16)
            return carry

        each(count, 16, body)

    def weight_terms(start, count, first):
        rows = pl.ds(start, count)
        for a, (left, right) in enumerate(((geps, h0), (xn0, gh0))):
            def body(i, carry):
                cols = pl.ds(pl.multiple_of(i * 256, 256), 256)
                term = tn(left[rows, cols], right[rows, :])
                if first:
                    acc[a, cols, :] = term
                else:
                    acc[a, cols, :] += term
                return carry

            lax.fori_loop(0, width // 256, body, None)

    hidden_back(*arrived(0))
    for step in range(1, 5):
        gather_step(2, geps, step)
        hidden_back(*arrived(step))
        if step == 2:
            weight_terms(4 * tok, 4 * tok, True)
    weight_terms(0, 4 * tok, False)

    def rows_of(a, slab, j, which):
        cx, cy = (slab, j) if a == 0 else (j, slab)
        return pl.ds(pl.multiple_of((cy // 2) * 640 + cx * 160 + (cy % 2) * 80 + which * 40, 40), 40)

    def pair(a, slab, part, which):
        return jnp.concatenate(
            [acc[a, rows_of(a, slab, 2 * part + j, which), :] for j in (0, 1)], axis=0
        )

    place = (x, y)
    along = (at_x, at_y)

    def core_copy(a, n):
        slab = (place[a] + (2, 1, 3, 0)[n]) % NR
        return remote(cstg.at[a, slab], crcv.at[a, slab], c_send.at[a, n], c_recv.at[a, n], partner)

    for n in range(4):
        for a in (0, 1):
            slab = (place[a] + (2, 1, 3, 0)[n]) % NR
            for part in (0, 1):
                cstg[a, slab, pl.ds(80 * part, 80), :] = pair(a, slab, part, 1 - core).astype(BF16)
            go(core_copy(a, n))

    def own_part(a, distance, part):
        slab = (place[a] + distance) % NR
        return pair(a, slab, part, core) + crcv[a, slab, pl.ds(80 * part, 80), :].astype(F32)

    def ring_copy(a, way, step, part):
        at = (a, way, 2 * (step - 1) + part)
        rows = pl.ds(80 * part, 80)
        return remote(
            rstg.at[a, way, step - 1, rows], rrcv.at[a, way, step - 1, rows],
            g_send.at[at], g_recv.at[at], along[a](1 if way == 0 else -1),
        )

    for a in (0, 1):
        core_copy(a, 0).wait_recv()
        for way in (0, 1):
            rstg[a, way, 0, pl.ds(80 * way, 80), :] = own_part(a, 2, way).astype(BF16)
            go(ring_copy(a, way, 1, way))
    for a in (0, 1):
        for way in (0, 1):
            core_copy(a, 1 + way).wait_recv()
            for part in (1 - way, way):
                value = own_part(a, 1 if way == 0 else 3, part)
                if part == way:
                    ring_copy(a, way, 1, part).wait_recv()
                    value = value + rrcv[a, way, 0, pl.ds(80 * part, 80), :].astype(F32)
                rstg[a, way, 1, pl.ds(80 * part, 80), :] = value.astype(BF16)
                go(ring_copy(a, way, 2, part))

    def last_copy(a, k):
        target = (place[1 - a] + k) % NR
        return remote(
            tstg.at[a, target], trcv.at[a, k - 1], t_send.at[a, k - 1], t_recv.at[a, k - 1],
            along[1 - a](k),
        )

    for a in (0, 1):
        core_copy(a, 3).wait_recv()
        for part in (0, 1):
            value = own_part(a, 0, part)
            for way in (0, 1):
                ring_copy(a, way, 2, part).wait_recv()
                value = value + rrcv[a, way, 1, pl.ds(80 * part, 80), :].astype(F32)
            for j in (0, 1):
                rows = value[40 * j:40 * j + 40]
                tsum[a, 2 * part + j] = rows
                tstg[a, 2 * part + j] = jnp.concatenate(
                    [rows, jnp.zeros((8, hidden), F32)], axis=0
                ).astype(BF16)
        for k in range(1, NR):
            go(last_copy(a, k))
    for a, result in enumerate((gout, gin)):
        total = tsum[a, place[1 - a]]
        for k in range(1, NR):
            last_copy(a, k).wait_recv()
            total = total + trcv[a, k - 1].astype(F32)[:40]
        result[...] = total
    for copy in pending:
        copy.wait_send()


def on_device(latents, timesteps, prompt_ids, prompt_table, gains, w_in, w_out):
    tok, width = latents.shape[1:]
    hidden = w_in.shape[2]
    rows = NZ * tok
    vmem, dma = pltpu.VMEM, pltpu.SemaphoreType.DMA
    scratch = [
        vmem((2, width, hidden), BF16),
        vmem((2, width, hidden), BF16),
        vmem((rows, width), BF16),
        vmem((rows, width), BF16),
        vmem((rows, hidden), BF16),
        vmem((rows, hidden), F32),
        vmem((rows, width), BF16),
        vmem((rows, width), BF16),
        vmem((rows, hidden), F32),
        vmem((rows, hidden), BF16),
        vmem((rows, width), BF16),
        vmem((rows, hidden), BF16),
        vmem((2 * tok, hidden), F32),
        vmem((2 * tok, width), F32),
        vmem((tok, width), F32),
        vmem((2, 4, tok, width), BF16),
        vmem((2, 4, tok, width), BF16),
        vmem((2, 4, tok, width), BF16),
        vmem((2, 4, tok, width), BF16),
        vmem((NZ, 8, 128), jnp.int32),
        vmem((NZ, hidden), F32),
        vmem((NZ, width), F32),
        vmem((2 * NZ, width // 2), BF16),
        vmem((NZ - 1, 2 * NZ, width // 2), BF16),
        vmem((2, width, hidden), F32),
        vmem((2, NR, 160, hidden), BF16),
        vmem((2, NR, 160, hidden), BF16),
        vmem((2, 2, 2, 160, hidden), BF16),
        vmem((2, 2, 2, 160, hidden), BF16),
        vmem((2, NR, 48, hidden), BF16),
        vmem((2, NR, 40, hidden), F32),
        vmem((2, NR - 1, 48, hidden), BF16),
        dma((3,)),
        dma((2, 8)), dma((2, 8)),
        dma((3, 2, 8)), dma((3, 2, 8)),
        dma((2, 2, 8)), dma((2, 2, 8)),
        dma((7,)), dma((7,)),
        dma((7,)), dma((7,)),
        dma((2, 4)), dma((2, 4)),
        dma((2, 2, 4)), dma((2, 2, 4)),
        dma((2, 3)), dma((2, 3)),
    ]
    whole, scalar, away = (pl.BlockSpec(memory_space=s) for s in (pltpu.VMEM, pltpu.SMEM, pl.ANY))
    share = jax.ShapeDtypeStruct((width // 32, hidden), F32)
    return pl.pallas_call(
        kernel,
        out_shape=(share, share),
        in_specs=[away, scalar, scalar, whole, whole, away, away],
        out_specs=(whole, whole),
        scratch_shapes=scratch,
        compiler_params=pltpu.CompilerParams(
            collective_id=0, has_side_effects=True, vmem_limit_bytes=56 * 2**20
        ),
        name="draft_step",
    )(latents, timesteps, prompt_ids, prompt_table, gains, w_in, w_out)


def solution(mesh):
    in_specs = (
        P(("dp", "tp"), None, None),
        P(("dp", "tp")),
        P(("dp", "tp")),
        P(),
        P(),
        P("sec", None, "tp"),
        P("sec", None, "tp"),
    )
    out_specs = (P(("sec", "dp"), "tp"), P(("sec", "dp"), "tp"))
    return jax.shard_map(
        on_device, mesh=mesh, in_specs=in_specs, out_specs=out_specs, check_vma=False
    )
```

```python
import functools
import math

import jax
import jax.numpy as jnp
from jax import lax
from jax.experimental import pallas as pl
from jax.experimental.pallas import tpu as pltpu
from jax.sharding import PartitionSpec as P

STEPS = 50
EPS = 1e-06
MESH = pl.DeviceIdType.MESH
F32, BF16 = jnp.float32, jnp.bfloat16

ORDER = (4, 5, 3, 6, 2, 7, 1, 0)
POS = {slot: pos for pos, slot in enumerate(ORDER)}
NZ, NR = 8, 4
PARTS = 4


def gelu_and_slope(value):
    cdf = 0.5 * (1.0 + lax.erf(value * (1.0 / math.sqrt(2.0))))
    pdf = jnp.exp(-0.5 * value * value) * (1.0 / math.sqrt(2.0 * math.pi))
    return value * cdf, cdf + value * pdf


def nt(left, right):
    return lax.dot_general(left, right, (((1,), (1,)), ((), ())), preferred_element_type=F32)


def tn(left, right):
    return lax.dot_general(left, right, (((0,), (0,)), ((), ())), preferred_element_type=F32)


def kernel(
    lat, steps, ids, table, gains, win, wout, gin, gout,
    w_in, w_out, lats, xn0, h0, sl0, imgs, xn1, sl1, gh1, geps, gh0, hp, pf, pf2, stg1, rcv1, stg2,
    rcv2, idb, hm, pm, pmsg, prcv, acc, cstg, crcv, rstg, rrcv, tstg, tsum, trcv,
    local_sem, w_send, w_recv, ag_send, ag_recv, rs_send, rs_recv, id_send, id_recv, p_send, p_recv,
    c_send, c_recv, g_send, g_recv, t_send, t_recv,
):
    tok, width = lat.shape[1], lat.shape[2]
    size = tok // PARTS
    hidden = win.shape[2]
    sec, dp, me = lax.axis_index("sec"), lax.axis_index("dp"), lax.axis_index("tp")
    x, ylo, core = dp // 4, (dp // 2) % 2, dp % 2
    y = sec * 2 + ylo
    other = 1 - sec

    def at_z(distance):
        return {"tp": (me + distance + NZ) % NZ}

    def at_x(distance):
        return {"dp": ((x + distance + NR) % NR) * 4 + ylo * 2 + core}

    def at_y(distance):
        there = (y + distance + NR) % NR
        return {"sec": there // 2, "dp": x * 4 + (there % 2) * 2 + core}

    partner = {"dp": x * 4 + ylo * 2 + (1 - core)}
    across = {"sec": other, "dp": x * 4 + (1 - ylo) * 2 + core}

    def remote(src, dst, send_sem, recv_sem, device):
        return pltpu.make_async_remote_copy(
            src_ref=src, dst_ref=dst, send_sem=send_sem, recv_sem=recv_sem,
            device_id=device, device_id_type=MESH,
        )

    def sent(ref, send_sem):
        remote(ref, ref, send_sem, c_recv.at[0, 0], partner).wait_send()

    here = [
        pltpu.make_async_copy(lat.at[sec], lats.at[pl.ds(POS[0] * tok, tok)], local_sem.at[0]),
        pltpu.make_async_copy(win.at[0], w_in.at[sec], local_sem.at[1]),
        pltpu.make_async_copy(wout.at[0], w_out.at[sec], local_sem.at[2]),
    ]
    for copy in here:
        copy.start()
    idb[0] = jnp.full((8, 128), ids[sec], jnp.int32)

    peers = [at_z(k) for k in range(1, NZ)] + [partner]
    peers += [at_x(k) for k in range(1, NR)] + [at_y(k) for k in range(1, NR)]
    barrier = pltpu.get_barrier_semaphore()
    for peer in peers:
        pl.semaphore_signal(barrier, inc=1, device_id=peer, device_id_type=MESH)
    pl.semaphore_wait(barrier, len(peers))

    def far(part, way):
        return part // (PARTS // 2) == way

    def parts_of(farthest):
        if farthest:
            return [(p + way * (PARTS // 2), way) for p in range(PARTS // 2) for way in (0, 1)]
        return [(part, way) for part in range(PARTS) for way in (0, 1)]

    def gather_copy(buf, way, step, part):
        if way == 0:
            src, dst, device = POS[step - 1], POS[step], at_z(1)
        else:
            src, dst, device = POS[(NZ - step + 1) % NZ], POS[NZ - step], at_z(-1)
        at = (way, PARTS * (step - 1) + part)
        return remote(
            buf.at[pl.ds(src * tok + part * size, size)],
            buf.at[pl.ds(dst * tok + part * size, size)],
            ag_send, ag_recv.at[at], device,
        )

    def gather_begin(buf, part):
        for way in (0, 1):
            gather_copy(buf, way, 1, part).start()

    def gather_step(buf, step):
        for part, way in parts_of(step == NZ // 2):
            gather_copy(buf, way, step, part).wait_recv()
            if step + 1 < NZ // 2 or (step + 1 == NZ // 2 and far(part, way)):
                gather_copy(buf, way, step + 1, part).start()

    def arrived(step):
        if step == 0:
            return POS[0] * tok, tok
        if step == NZ // 2:
            return 0, tok
        return POS[NZ - step] * tok, 2 * tok

    def scatter_copy(stg, rcv, way, step, part):
        at = (way, PARTS * (step - 1) + part)
        rows = pl.ds(part * size, size)
        return remote(
            stg.at[way, step - 1, rows], rcv.at[way, step - 1, rows],
            rs_send, rs_recv.at[at], at_z(1) if way == 0 else at_z(-1),
        )

    def scatter_step(stg, rcv, step):
        rows = parts_of(step == 1)
        if step == 2:
            rows.sort(key=lambda row: far(*row))
        for part, way in rows:
            at = pl.ds(part * size, size)
            base = part * size + (way * tok if step > 1 else 0)
            value = pf[pl.ds(base, size), :]
            if step > 2 or (step == 2 and far(part, way)):
                scatter_copy(stg, rcv, way, step - 1, part).wait_recv()
                value = value + rcv[way, step - 2, at, :].astype(F32)
            stg[way, step - 1, at, :] = value.astype(BF16)
            scatter_copy(stg, rcv, way, step, part).start()

    def scatter_end(stg, rcv, part):
        for way in (0, 1):
            scatter_copy(stg, rcv, way, NZ // 2, part).wait_recv()

    def chunk(step):
        return arrived(5 - step) if step > 1 else (0, tok)

    quarter = (x + 2 * ylo) % NR

    def piece(offset, which):
        rows = (quarter + offset) % NR * (width // NR) + which * (width // NR // 2)
        return pl.ds(pl.multiple_of(rows, 32), width // NR // 2)

    held = (w_in, w_out)
    given = (win, wout)
    beside = {"dp": x * 4 + (1 - ylo) * 2 + core}

    def weight_copy(a, kind):
        if kind == 0:
            rows = piece(2, core)
            src, dst, device = given[a].at[0, rows], held[a].at[sec, rows], across
        else:
            rows = piece((0, 0, 0, 0, 0, 3, 1, 2)[kind], core)
            src = dst = held[a].at[other, rows]
            device = (at_x(1), at_x(-1), beside, partner)[min(kind, 4) - 1]
        return remote(src, dst, w_send, w_recv.at[a, kind], device)

    def weight_landed(a, kind):
        ref = held[a].at[other, piece((0, 3, 1, 2)[kind % 4], core if kind < 4 else 1 - core)]
        remote(ref, ref, w_send, w_recv.at[a, kind], partner).wait_recv()

    def weights_first(a):
        weight_landed(a, 0)
        for kind in (1, 2, 3, 4):
            weight_copy(a, kind).start()

    def weights_second(a):
        for kind in (1, 2, 3):
            weight_landed(a, kind)
            weight_copy(a, kind + 4).start()

    def weights_last(a):
        for kind in (4, 5, 6, 7):
            weight_landed(a, kind)

    def each(count, rows, body, init=None):
        return lax.fori_loop(0, count // rows, lambda i, c: body(pl.multiple_of(i * rows, rows), c), init)

    def norm(buf, dst, start, count, gain, slots=None):
        def body(at, total):
            value = buf[pl.ds(start + at, 16), :].astype(F32)
            scale = lax.rsqrt(jnp.mean(value * value, axis=-1, keepdims=True) + EPS)
            dst[pl.ds(start + at, 16), :] = (value * scale * gain).astype(BF16)
            return None if total is None else total + value[:8] + value[8:]

        if slots is None:
            each(count, 16, body)
            return
        for index, slot in enumerate(slots):
            start = POS[slot] * tok
            total = each(tok, 16, body, jnp.zeros((8, width), F32))
            pm[pl.ds(slot, 1), :] = jnp.sum(total, axis=0, keepdims=True) * (1.0 / tok)

    def slots_of(start, count):
        return ORDER[start // tok:(start + count) // tok]

    theta = (jnp.full((1, 128), steps[sec], jnp.int32).astype(F32) + 1.0) * (
        math.pi / 2.0 / (STEPS + 1.0)
    )
    alpha, sigma = jnp.cos(theta)[:, :1], jnp.sin(theta)[:, :1]
    weight_copy(0, 0).start()
    weight_copy(1, 0).start()
    here[0].wait()
    for part in range(PARTS):
        gather_begin(lats, part)
    for k in range(1, NZ):
        remote(idb.at[0], idb.at[k], id_send, id_recv.at[k - 1], at_z(k)).start()
    gain0, gain1 = gains[0:1, :], gains[1:2, :]
    norm(lats, xn0, *arrived(0), gain0)
    gather_step(lats, 1)
    weights_first(0)
    norm(lats, xn0, *arrived(1), gain0)
    gather_step(lats, 2)
    norm(lats, xn0, *arrived(2), gain0)
    weights_first(1)
    gather_step(lats, 3)
    weights_second(0)
    norm(lats, xn0, *arrived(3), gain0)
    gather_step(lats, 4)
    norm(lats, xn0, *arrived(4), gain0)
    here[1].wait()
    weights_last(0)

    def hidden0(start, count):
        hp[pl.ds(0, count), :] = jnp.dot(
            xn0[pl.ds(start, count), :], w_in[0], preferred_element_type=F32
        )

        def body(at, carry):
            act, slope = gelu_and_slope(hp[pl.ds(at, 16), :])
            h0[pl.ds(start + at, 16), :] = act.astype(BF16)
            sl0[pl.ds(start + at, 16), :] = slope
            return carry

        each(count, 16, body)

    hidden0(*chunk(1))
    weights_second(1)
    hidden0(*chunk(2))
    here[2].wait()
    weights_last(1)

    for step in range(1, 6):
        start, count = chunk(step)
        if step > 2:
            hidden0(start, count)
        out = nt(h0[pl.ds(start, count), :], w_out[0])
        if step < 5:
            pf[pl.ds(0, count), :] = out
            scatter_step(stg1, rcv1, step)
        else:
            pf2[...] = out

    own = POS[0] * tok
    sent(lats.at[pl.ds(0, (NZ - 1) * tok)], ag_send)
    for part in range(PARTS):
        scatter_end(stg1, rcv1, part)

        def images(at, carry):
            rows = pl.ds(part * size + at, 16)
            base = lats[pl.ds(own + part * size + at, 16), :].astype(F32)
            mix = pf2[rows, :] + (rcv1[0, 3, rows, :].astype(F32) + rcv1[1, 3, rows, :].astype(F32))
            imgs[pl.ds(own + part * size + at, 16), :] = (
                (base - sigma * (base + mix)) / alpha
            ).astype(BF16)
            return carry

        each(size, 16, images)
        gather_begin(imgs, part)

    def hidden1(start, count):
        slots = slots_of(start, count)
        norm(imgs, xn1, start, count, gain1, slots)
        hp[pl.ds(0, count), :] = jnp.dot(
            xn1[pl.ds(start, count), :], w_in[1], preferred_element_type=F32
        )
        for index, slot in enumerate(slots):
            def body(at, total):
                act, slope = gelu_and_slope(hp[pl.ds(index * tok + at, 16), :])
                sl1[pl.ds(start + index * tok + at, 16), :] = slope
                act = act.astype(BF16).astype(F32)
                return total + act[:8] + act[8:]

            total = each(tok, 16, body, jnp.zeros((8, hidden), F32))
            hm[pl.ds(slot, 1), :] = jnp.sum(total, axis=0, keepdims=True) * (1.0 / tok)

    hidden1(*arrived(0))
    for k in range(1, NZ):
        remote(idb.at[k], idb.at[k], id_send, id_recv.at[k - 1], at_z(k)).wait_recv()
    id_rows = jnp.concatenate([idb[k, 0:1, :] for k in range(NZ)], axis=0)
    prompts = table.shape[0]
    onehot = (
        id_rows[:, :prompts] == lax.broadcasted_iota(jnp.int32, (NZ, prompts), 1)
    ).astype(F32).astype(BF16)
    text = jnp.dot(onehot, table[...], preferred_element_type=F32)
    text = text * lax.rsqrt(jnp.mean(text * text, axis=-1, keepdims=True) + EPS)
    for step in range(1, 5):
        gather_step(imgs, step)
        hidden1(*arrived(step))

    mean1 = hm[...]
    high = mean1.astype(BF16).astype(F32)
    both = jnp.concatenate([high, mean1 - high], axis=0).astype(BF16)
    mixed = nt(both, w_out[1])
    mixed = mixed[:NZ] + mixed[NZ:]
    mid = width // 2
    pmsg[...] = jnp.concatenate([mixed[:, :mid], mixed[:, mid:]], axis=0).astype(BF16)
    for k in range(1, NZ):
        remote(pmsg, prcv.at[k - 1], p_send, p_recv.at[k - 1], at_z(k)).start()
    pooled = pm[...] + mixed
    for k in range(1, NZ):
        remote(pmsg, prcv.at[k - 1], p_send, p_recv.at[k - 1], at_z(k)).wait_recv()
        got = prcv[k - 1].astype(F32)
        got = jnp.concatenate([got[:NZ], got[NZ:]], axis=1)
        pooled = pooled + jnp.concatenate([got[NZ - k:], got[:NZ - k]], axis=0)
    unit = lax.rsqrt(jnp.mean(pooled * pooled, axis=-1, keepdims=True) + EPS)
    g_mean = (unit * text - pooled * (unit * unit * unit) * jnp.mean(
        pooled * text, axis=-1, keepdims=True
    )) * (-100.0 / width / tok)
    g_h1 = jnp.dot(g_mean.astype(BF16), w_out[1], preferred_element_type=F32)
    g_own = g_mean[0:1, :]
    sent(lats.at[pl.ds(0, (NZ - 1) * tok)], rs_send)

    for step in range(1, 6):
        start, count = chunk(step)
        for index, slot in enumerate(slots_of(start, count)):
            row = g_h1[slot:slot + 1, :]

            def slope_times(at, carry):
                rows = pl.ds(start + index * tok + at, 16)
                gh1[rows, :] = (row * sl1[rows, :]).astype(BF16)
                return carry

            each(tok, 16, slope_times)
        out = nt(gh1[pl.ds(start, count), :], w_in[1])
        if step < 5:
            pf[pl.ds(0, count), :] = out
            scatter_step(stg2, rcv2, step)
        else:
            pf2[...] = out

    ratio = -(sigma / alpha)
    sent(lats.at[pl.ds(0, (NZ - 1) * tok)], ag_send)
    for part in range(PARTS):
        scatter_end(stg2, rcv2, part)

        def back(at, carry):
            rows = pl.ds(part * size + at, 16)
            seen = imgs[pl.ds(own + part * size + at, 16), :].astype(F32)
            g_xn = pf2[rows, :] + (
                rcv2[0, 3, rows, :].astype(F32) + rcv2[1, 3, rows, :].astype(F32)
            )
            scale = lax.rsqrt(jnp.mean(seen * seen, axis=-1, keepdims=True) + EPS)
            weighted = gain1 * g_xn
            g_norm = scale * weighted - seen * (scale * scale * scale) * jnp.mean(
                seen * weighted, axis=-1, keepdims=True
            )
            g_images = (g_own + g_norm).astype(BF16).astype(F32)
            geps[pl.ds(own + part * size + at, 16), :] = (ratio * g_images).astype(BF16)
            return carry

        each(size, 16, back)
        gather_begin(geps, part)

    def hidden_back(start, count):
        hp[pl.ds(0, count), :] = jnp.dot(
            geps[pl.ds(start, count), :], w_out[0], preferred_element_type=F32
        )

        def body(at, carry):
            rows = pl.ds(start + at, 16)
            gh0[rows, :] = (hp[pl.ds(at, 16), :] * sl0[rows, :]).astype(BF16)
            return carry

        each(count, 16, body)

    def weight_terms(a, start, count, first):
        left, right = ((geps, h0), (xn0, gh0))[a]
        rows = pl.ds(start, count)

        def body(i, carry):
            cols = pl.ds(pl.multiple_of(i * 256, 256), 256)
            term = tn(left[rows, cols], right[rows, :])
            if first:
                acc[a, cols, :] = term
            else:
                acc[a, cols, :] += term
            return carry

        lax.fori_loop(0, width // 256, body, None)

    def rows_of(a, slab, j, which):
        cx, cy = (slab, j) if a == 0 else (j, slab)
        return pl.ds(pl.multiple_of((cy // 2) * 640 + cx * 160 + (cy % 2) * 80 + which * 40, 40), 40)

    def pair(a, slab, part, which):
        return jnp.concatenate(
            [acc[a, rows_of(a, slab, 2 * part + j, which), :] for j in (0, 1)], axis=0
        )

    place = (x, y)
    along = (at_x, at_y)

    def core_copy(a, n):
        slab = (place[a] + (2, 1, 3, 0)[n]) % NR
        return remote(cstg.at[a, slab], crcv.at[a, slab], c_send, c_recv.at[a, n], partner)

    def core_send(a):
        for n in range(4):
            slab = (place[a] + (2, 1, 3, 0)[n]) % NR
            for part in (0, 1):
                cstg[a, slab, pl.ds(80 * part, 80), :] = pair(a, slab, part, 1 - core).astype(BF16)
            core_copy(a, n).start()

    hidden_back(*arrived(0))
    for step in range(1, 5):
        gather_step(geps, step)
        if step < 4:
            hidden_back(*arrived(step))
        if step == 3:
            weight_terms(0, tok, 7 * tok, True)
            weight_terms(1, tok, 7 * tok, True)
    weight_terms(0, 0, tok, False)
    core_send(0)
    hidden_back(*arrived(4))
    weight_terms(1, 0, tok, False)
    core_send(1)

    def own_part(a, distance, part):
        slab = (place[a] + distance) % NR
        return pair(a, slab, part, core) + crcv[a, slab, pl.ds(80 * part, 80), :].astype(F32)

    def ring_copy(a, way, step, part):
        at = (a, way, 2 * (step - 1) + part)
        rows = pl.ds(80 * part, 80)
        return remote(
            rstg.at[a, way, step - 1, rows], rrcv.at[a, way, step - 1, rows],
            g_send, g_recv.at[at], along[a](1 if way == 0 else -1),
        )

    for a in (0, 1):
        core_copy(a, 0).wait_recv()
        for way in (0, 1):
            rstg[a, way, 0, pl.ds(80 * way, 80), :] = own_part(a, 2, way).astype(BF16)
            ring_copy(a, way, 1, way).start()
    for a in (0, 1):
        for way in (0, 1):
            core_copy(a, 1 + way).wait_recv()
            for part in (1 - way, way):
                value = own_part(a, 1 if way == 0 else 3, part)
                if part == way:
                    ring_copy(a, way, 1, part).wait_recv()
                    value = value + rrcv[a, way, 0, pl.ds(80 * part, 80), :].astype(F32)
                rstg[a, way, 1, pl.ds(80 * part, 80), :] = value.astype(BF16)
                ring_copy(a, way, 2, part).start()

    def last_copy(a, k):
        target = (place[1 - a] + k) % NR
        return remote(
            tstg.at[a, target], trcv.at[a, k - 1], t_send, t_recv.at[a, k - 1],
            along[1 - a](k),
        )

    for a in (0, 1):
        core_copy(a, 3).wait_recv()
        for part in (0, 1):
            value = own_part(a, 0, part)
            for way in (0, 1):
                ring_copy(a, way, 2, part).wait_recv()
                value = value + rrcv[a, way, 1, pl.ds(80 * part, 80), :].astype(F32)
            for j in (0, 1):
                rows = value[40 * j:40 * j + 40]
                tsum[a, 2 * part + j] = rows
                tstg[a, 2 * part + j] = jnp.concatenate(
                    [rows, jnp.zeros((8, hidden), F32)], axis=0
                ).astype(BF16)
        for k in range(1, NR):
            last_copy(a, k).start()
    for a, result in enumerate((gout, gin)):
        total = tsum[a, place[1 - a]]
        for k in range(1, NR):
            last_copy(a, k).wait_recv()
            total = total + trcv[a, k - 1].astype(F32)[:40]
        result[...] = total
    sent(lats.at[pl.ds(0, (NZ - 1) * tok)], ag_send)
    sent(lats.at[pl.ds(0, (NZ - 1) * tok)], rs_send)
    sent(w_in, w_send)
    sent(idb.at[pl.ds(0, NZ - 1)], id_send)
    sent(prcv, p_send)
    sent(crcv, c_send)
    sent(w_in.at[0, pl.ds(0, 960)], g_send)
    sent(trcv, t_send)


def hand_over(left, right, left_out, right_out):
    left_out[...] = left[...]
    right_out[...] = right[...]


def on_device(latents, timesteps, prompt_ids, prompt_table, gains, w_in, w_out):
    tok, width = latents.shape[1:]
    hidden = w_in.shape[2]
    rows = NZ * tok
    vmem, dma = pltpu.VMEM, pltpu.SemaphoreType.DMA
    scratch = [
        vmem((2, width, hidden), BF16),
        vmem((2, width, hidden), BF16),
        vmem((rows, width), BF16),
        vmem((rows, width), BF16),
        vmem((rows, hidden), BF16),
        vmem((rows, hidden), F32),
        vmem((rows, width), BF16),
        vmem((rows, width), BF16),
        vmem((rows, hidden), F32),
        vmem((rows, hidden), BF16),
        vmem((rows, width), BF16),
        vmem((rows, hidden), BF16),
        vmem((2 * tok, hidden), F32),
        vmem((2 * tok, width), F32),
        vmem((tok, width), F32),
        vmem((2, 4, tok, width), BF16),
        vmem((2, 4, tok, width), BF16),
        vmem((2, 4, tok, width), BF16),
        vmem((2, 4, tok, width), BF16),
        vmem((NZ, 8, 128), jnp.int32),
        vmem((NZ, hidden), F32),
        vmem((NZ, width), F32),
        vmem((2 * NZ, width // 2), BF16),
        vmem((NZ - 1, 2 * NZ, width // 2), BF16),
        vmem((2, width, hidden), F32),
        vmem((2, NR, 160, hidden), BF16),
        vmem((2, NR, 160, hidden), BF16),
        vmem((2, 2, 2, 160, hidden), BF16),
        vmem((2, 2, 2, 160, hidden), BF16),
        vmem((2, NR, 48, hidden), BF16),
        vmem((2, NR, 40, hidden), F32),
        vmem((2, NR - 1, 48, hidden), BF16),
        dma((3,)),
        dma(()), dma((2, 8)),
        dma(()), dma((2, 4 * PARTS)),
        dma(()), dma((2, 4 * PARTS)),
        dma(()), dma((7,)),
        dma(()), dma((7,)),
        dma(()), dma((2, 4)),
        dma(()), dma((2, 2, 4)),
        dma(()), dma((2, 3)),
    ]
    whole, scalar, away = (pl.BlockSpec(memory_space=s) for s in (pltpu.VMEM, pltpu.SMEM, pl.ANY))
    share = jax.ShapeDtypeStruct((width // 32, hidden), F32)
    shares = pl.pallas_call(
        kernel,
        out_shape=(share, share),
        in_specs=[away, scalar, scalar, whole, whole, away, away],
        out_specs=(whole, whole),
        scratch_shapes=scratch,
        compiler_params=pltpu.CompilerParams(
            collective_id=0, has_side_effects=True, vmem_limit_bytes=56 * 2**20
        ),
        name="draft_step",
    )(latents, timesteps, prompt_ids, prompt_table, gains, w_in, w_out)
    return pl.pallas_call(hand_over, out_shape=(share, share), name="hand_over")(*shares)


def solution(mesh):
    in_specs = (
        P(("dp", "tp"), None, None),
        P(("dp", "tp")),
        P(("dp", "tp")),
        P(),
        P(),
        P("sec", None, "tp"),
        P("sec", None, "tp"),
    )
    out_specs = (P(("sec", "dp"), "tp"), P(("sec", "dp"), "tp"))
    return jax.shard_map(
        on_device, mesh=mesh, in_specs=in_specs, out_specs=out_specs, check_vma=False
    )
```

```python
import functools
import math

import jax
import jax.numpy as jnp
from jax import lax
from jax.experimental import pallas as pl
from jax.experimental.pallas import tpu as pltpu
from jax.sharding import PartitionSpec as P

STEPS = 50
EPS = 1e-06
MESH = pl.DeviceIdType.MESH
F32, BF16 = jnp.float32, jnp.bfloat16

ORDER = (4, 5, 3, 6, 2, 7, 1, 0)
POS = {slot: pos for pos, slot in enumerate(ORDER)}
NZ, NR = 8, 4
PARTS = 4


def gelu_and_slope(value):
    cdf = 0.5 * (1.0 + lax.erf(value * (1.0 / math.sqrt(2.0))))
    pdf = jnp.exp(-0.5 * value * value) * (1.0 / math.sqrt(2.0 * math.pi))
    return value * cdf, cdf + value * pdf


def nt(left, right):
    return lax.dot_general(left, right, (((1,), (1,)), ((), ())), preferred_element_type=F32)


def tn(left, right):
    return lax.dot_general(left, right, (((0,), (0,)), ((), ())), preferred_element_type=F32)


def kernel(
    lat, steps, ids, table, gains, win, wout, gin, gout,
    w_in, w_out, lats, xn0, h0, sl0, imgs, xn1, sl1, gh1, geps, gh0, hp, pf, pf2, stg1, rcv1, stg2,
    rcv2, idb, hm, pm, pmsg, prcv, pmsg2, prcv2, acc, turned, cstg, crcv, rstg, rrcv, tstg, tsum, trcv,
    local_sem, w_send, w_recv, ag_send, ag_recv, rs_send, rs_recv, id_send, id_recv, p_send, p_recv, p2_send, p2_recv,
    c_send, c_recv, g_send, g_recv, t_send, t_recv,
):
    tok, width = lat.shape[1], lat.shape[2]
    size = tok // PARTS
    hidden = win.shape[2]
    sec, dp, me = lax.axis_index("sec"), lax.axis_index("dp"), lax.axis_index("tp")
    x, ylo, core = dp // 4, (dp // 2) % 2, dp % 2
    y = sec * 2 + ylo
    other = 1 - sec

    def at_z(distance):
        return {"tp": (me + distance + NZ) % NZ}

    def at_x(distance):
        return {"dp": ((x + distance + NR) % NR) * 4 + ylo * 2 + core}

    def at_y(distance):
        there = (y + distance + NR) % NR
        return {"sec": there // 2, "dp": x * 4 + (there % 2) * 2 + core}

    partner = {"dp": x * 4 + ylo * 2 + (1 - core)}
    across = {"sec": other, "dp": x * 4 + (1 - ylo) * 2 + core}

    def remote(src, dst, send_sem, recv_sem, device):
        return pltpu.make_async_remote_copy(
            src_ref=src, dst_ref=dst, send_sem=send_sem, recv_sem=recv_sem,
            device_id=device, device_id_type=MESH,
        )

    def sent(ref, send_sem):
        remote(ref, ref, send_sem, c_recv.at[0, 0], partner).wait_send()

    here = [
        pltpu.make_async_copy(lat.at[sec], lats.at[pl.ds(POS[0] * tok, tok)], local_sem.at[0]),
        pltpu.make_async_copy(win.at[0], w_in.at[sec], local_sem.at[1]),
        pltpu.make_async_copy(wout.at[0], w_out.at[sec], local_sem.at[2]),
    ]
    for copy in here:
        copy.start()
    idb[0] = jnp.full((8, 128), ids[sec], jnp.int32)

    peers = [at_z(k) for k in range(1, NZ)] + [partner]
    peers += [at_x(k) for k in range(1, NR)] + [at_y(k) for k in range(1, NR)]
    barrier = pltpu.get_barrier_semaphore()
    for peer in peers:
        pl.semaphore_signal(barrier, inc=1, device_id=peer, device_id_type=MESH)
    pl.semaphore_wait(barrier, len(peers))

    def far(part, way):
        return part // (PARTS // 2) == way

    far_parts = [(p + way * (PARTS // 2), way) for p in range(PARTS // 2) for way in (0, 1)]
    near_parts = [(p + (1 - way) * (PARTS // 2), way) for p in range(PARTS // 2) for way in (0, 1)]

    def gather_copy(buf, way, step, part):
        if way == 0:
            src, dst, device = POS[step - 1], POS[step], at_z(1)
        else:
            src, dst, device = POS[(NZ - step + 1) % NZ], POS[NZ - step], at_z(-1)
        at = (way, PARTS * (step - 1) + part)
        return remote(
            buf.at[pl.ds(src * tok + part * size, size)],
            buf.at[pl.ds(dst * tok + part * size, size)],
            ag_send, ag_recv.at[at], device,
        )

    def gather_begin(buf, parts):
        for part, way in parts:
            gather_copy(buf, way, 1, part).start()

    def gather_parts(buf, step, parts):
        for part, way in parts:
            gather_copy(buf, way, step, part).wait_recv()
            if step + 1 < NZ // 2 or (step + 1 == NZ // 2 and far(part, way)):
                gather_copy(buf, way, step + 1, part).start()

    def gather_step(buf, step):
        gather_parts(buf, step, far_parts)
        if step < NZ // 2:
            gather_parts(buf, step, near_parts)

    def gather_with(buf, work, middle=None):
        work(*arrived(0))
        gather_step(buf, 1)
        for step in (1, 2, 3):
            start, count = arrived(step)
            work(start, tok)
            if step < 3:
                gather_parts(buf, step + 1, far_parts)
            work(start + tok, tok)
            if step == 2 and middle is not None:
                middle()
            if step < 3:
                gather_parts(buf, step + 1, near_parts)

    def arrived(step):
        if step == 0:
            return POS[0] * tok, tok
        if step == NZ // 2:
            return 0, tok
        return POS[NZ - step] * tok, 2 * tok

    def scatter_copy(stg, rcv, way, step, part):
        at = (way, PARTS * (step - 1) + part)
        rows = pl.ds(part * size, size)
        return remote(
            stg.at[way, step - 1, rows], rcv.at[way, step - 1, rows],
            rs_send, rs_recv.at[at], at_z(1) if way == 0 else at_z(-1),
        )

    def scatter_step(stg, rcv, step):
        for part, way in (near_parts if step > 1 else []) + far_parts:
            at = pl.ds(part * size, size)
            base = part * size + (way * tok if step > 1 else 0)
            value = pf[pl.ds(base, size), :]
            if step > 2 or (step == 2 and far(part, way)):
                scatter_copy(stg, rcv, way, step - 1, part).wait_recv()
                value = value + rcv[way, step - 2, at, :].astype(F32)
            stg[way, step - 1, at, :] = value.astype(BF16)
            scatter_copy(stg, rcv, way, step, part).start()

    def scatter_end(stg, rcv, part):
        for way in (0, 1):
            scatter_copy(stg, rcv, way, NZ // 2, part).wait_recv()

    def chunk(step):
        return arrived(5 - step) if step > 1 else (0, tok)

    quarter = (x + 2 * ylo) % NR

    def piece(offset, which, h):
        rows = (quarter + offset) % NR * (width // NR) + which * (width // NR // 2)
        return pl.ds(pl.multiple_of(rows + h * (width // NR // 4), 16), width // NR // 4)

    held = (w_in, w_out)
    given = (win, wout)
    beside = {"dp": x * 4 + (1 - ylo) * 2 + core}

    def weight_copy(a, kind, h):
        if kind == 0:
            rows = piece(2, core, h)
            src, dst, device = given[a].at[0, rows], held[a].at[sec, rows], across
        else:
            rows = piece((0, 0, 0, 0, 0, 3, 1, 2)[kind], core, h)
            src = dst = held[a].at[other, rows]
            device = (at_x(1), at_x(-1), beside, partner)[min(kind, 4) - 1]
        return remote(src, dst, w_send, w_recv.at[a, kind, h], device)

    def weight_landed(a, kind, h):
        ref = held[a].at[other, piece((0, 3, 1, 2)[kind % 4], core if kind < 4 else 1 - core, h)]
        remote(ref, ref, w_send, w_recv.at[a, kind, h], partner).wait_recv()

    def weights_first(a, h):
        weight_landed(a, 0, h)
        for kind in (1, 2, 3, 4):
            weight_copy(a, kind, h).start()

    def weights_second(a, h):
        for kind in (1, 2, 3):
            weight_landed(a, kind, h)
            weight_copy(a, kind + 4, h).start()

    def weights_last(a):
        for h in (0, 1):
            for kind in (4, 5, 6, 7):
                weight_landed(a, kind, h)

    def each(count, rows, body, init=None):
        return lax.fori_loop(0, count // rows, lambda i, c: body(pl.multiple_of(i * rows, rows), c), init)

    def norm(buf, dst, start, count, gain, slots=None):
        def body(at, total):
            value = buf[pl.ds(start + at, 16), :].astype(F32)
            scale = lax.rsqrt(jnp.mean(value * value, axis=-1, keepdims=True) + EPS)
            dst[pl.ds(start + at, 16), :] = (value * scale * gain).astype(BF16)
            return None if total is None else total + value[:8] + value[8:]

        if slots is None:
            each(count, 16, body)
            return
        for index, slot in enumerate(slots):
            start = POS[slot] * tok
            total = each(tok, 16, body, jnp.zeros((8, width), F32))
            pm[pl.ds(slot, 1), :] = jnp.sum(total, axis=0, keepdims=True) * (1.0 / tok)

    def slots_of(start, count):
        return ORDER[start // tok:(start + count) // tok]

    theta = (jnp.full((1, 128), steps[sec], jnp.int32).astype(F32) + 1.0) * (
        math.pi / 2.0 / (STEPS + 1.0)
    )
    alpha, sigma = jnp.cos(theta)[:, :1], jnp.sin(theta)[:, :1]
    for a in (0, 1):
        for h in (0, 1):
            weight_copy(a, 0, h).start()
    here[0].wait()
    gather_begin(lats, far_parts + near_parts)
    for k in range(1, NZ):
        remote(idb.at[0], idb.at[k], id_send, id_recv.at[k - 1], at_z(k)).start()
    gain0, gain1 = gains[0:1, :], gains[1:2, :]
    norm(lats, xn0, *arrived(0), gain0)
    gather_step(lats, 1)
    weights_first(0, 0)
    norm(lats, xn0, *arrived(1), gain0)
    weights_first(0, 1)
    gather_step(lats, 2)
    weights_first(1, 0)
    weights_second(0, 0)
    norm(lats, xn0, *arrived(2), gain0)
    weights_first(1, 1)
    weights_second(0, 1)
    gather_step(lats, 3)
    weights_second(1, 0)
    norm(lats, xn0, *arrived(3), gain0)
    gather_step(lats, 4)
    weights_second(1, 1)
    norm(lats, xn0, *arrived(4), gain0)
    here[1].wait()
    weights_last(0)

    def hidden0(start, count):
        hp[pl.ds(0, count), :] = jnp.dot(
            xn0[pl.ds(start, count), :], w_in[0], preferred_element_type=F32
        )

        def body(at, carry):
            act, slope = gelu_and_slope(hp[pl.ds(at, 16), :])
            h0[pl.ds(start + at, 16), :] = act.astype(BF16)
            sl0[pl.ds(start + at, 16), :] = slope
            return carry

        each(count, 16, body)

    hidden0(*chunk(1))
    here[2].wait()
    weights_last(1)

    for step in range(1, 6):
        start, count = chunk(step)
        if step > 1:
            hidden0(start, count)
        out = nt(h0[pl.ds(start, count), :], w_out[0])
        if step < 5:
            pf[pl.ds(0, count), :] = out
            scatter_step(stg1, rcv1, step)
        else:
            pf2[...] = out

    own = POS[0] * tok
    sent(lats.at[pl.ds(0, (NZ - 1) * tok)], ag_send)
    for part, way in far_parts:
        scatter_end(stg1, rcv1, part)

        def images(at, carry):
            rows = pl.ds(part * size + at, 16)
            base = lats[pl.ds(own + part * size + at, 16), :].astype(F32)
            mix = pf2[rows, :] + (rcv1[0, 3, rows, :].astype(F32) + rcv1[1, 3, rows, :].astype(F32))
            imgs[pl.ds(own + part * size + at, 16), :] = (
                (base - sigma * (base + mix)) / alpha
            ).astype(BF16)
            return carry

        each(size, 16, images)
        gather_begin(imgs, [(part, way)])

    gather_begin(imgs, near_parts)

    def hidden1(start, count):
        slots = slots_of(start, count)
        norm(imgs, xn1, start, count, gain1, slots)
        hp[pl.ds(0, count), :] = jnp.dot(
            xn1[pl.ds(start, count), :], w_in[1], preferred_element_type=F32
        )
        for index, slot in enumerate(slots):
            def body(at, total):
                act, slope = gelu_and_slope(hp[pl.ds(index * tok + at, 16), :])
                sl1[pl.ds(start + index * tok + at, 16), :] = slope
                act = act.astype(BF16).astype(F32)
                return total + act[:8] + act[8:]

            total = each(tok, 16, body, jnp.zeros((8, hidden), F32))
            hm[pl.ds(slot, 1), :] = jnp.sum(total, axis=0, keepdims=True) * (1.0 / tok)

    for k in range(1, NZ):
        remote(idb.at[k], idb.at[k], id_send, id_recv.at[k - 1], at_z(k)).wait_recv()
    id_rows = jnp.concatenate([idb[k, 0:1, :] for k in range(NZ)], axis=0)
    prompts = table.shape[0]
    onehot = (
        id_rows[:, :prompts] == lax.broadcasted_iota(jnp.int32, (NZ, prompts), 1)
    ).astype(F32).astype(BF16)
    text = jnp.dot(onehot, table[...], preferred_element_type=F32)
    text = text * lax.rsqrt(jnp.mean(text * text, axis=-1, keepdims=True) + EPS)
    def mixed_rows(rows):
        high = rows.astype(BF16).astype(F32)
        both = jnp.concatenate([high, rows - high], axis=0).astype(BF16)
        out = nt(both, w_out[1])
        return out[:NZ] + out[NZ:]

    def exchange(message, arrivals, send_sem, recv_sem, k):
        return remote(message, arrivals.at[k - 1], send_sem, recv_sem.at[k - 1], at_z(k))

    mid = width // 2
    opposite = NZ // 2
    hm[pl.ds(opposite, 1), :] = jnp.zeros((1, hidden), F32)
    gather_with(imgs, hidden1)
    mixed = mixed_rows(hm[...])
    pmsg[...] = jnp.concatenate([mixed[:, :mid], mixed[:, mid:]], axis=0).astype(BF16)
    for k in range(1, NZ):
        exchange(pmsg, prcv, p_send, p_recv, k).start()
    gather_parts(imgs, 4, far_parts)
    hidden1(*arrived(4))

    lanes = width // 128
    last = mixed_rows(jnp.broadcast_to(hm[pl.ds(opposite, 1), :], (NZ, hidden)))[0:1]
    pmsg2[...] = jnp.concatenate(
        [last[:, 128 * i:128 * i + 128] for i in range(lanes)] + [jnp.zeros((16 - lanes, 128), F32)],
        axis=0,
    ).astype(BF16)
    for k in range(1, NZ):
        exchange(pmsg2, prcv2, p2_send, p2_recv, k).start()
    pooled = pm[...] + mixed
    for k in range(1, NZ):
        exchange(pmsg, prcv, p_send, p_recv, k).wait_recv()
        got = prcv[k - 1].astype(F32)
        got = jnp.concatenate([got[:NZ], got[NZ:]], axis=1)
        pooled = pooled + jnp.concatenate([got[NZ - k:], got[:NZ - k]], axis=0)
    rows = {opposite: last}
    for k in range(1, NZ):
        exchange(pmsg2, prcv2, p2_send, p2_recv, k).wait_recv()
        got = prcv2[k - 1].astype(F32)
        rows[(opposite + k) % NZ] = jnp.concatenate([got[i:i + 1] for i in range(lanes)], axis=1)
    pooled = pooled + jnp.concatenate([rows[k] for k in range(NZ)], axis=0)
    unit = lax.rsqrt(jnp.mean(pooled * pooled, axis=-1, keepdims=True) + EPS)
    g_mean = (unit * text - pooled * (unit * unit * unit) * jnp.mean(
        pooled * text, axis=-1, keepdims=True
    )) * (-100.0 / width / tok)
    g_h1 = jnp.dot(g_mean.astype(BF16), w_out[1], preferred_element_type=F32)
    g_own = g_mean[0:1, :]
    sent(lats.at[pl.ds(0, (NZ - 1) * tok)], rs_send)

    for step in range(1, 6):
        start, count = chunk(step)
        for index, slot in enumerate(slots_of(start, count)):
            row = g_h1[slot:slot + 1, :]

            def slope_times(at, carry):
                rows = pl.ds(start + index * tok + at, 16)
                gh1[rows, :] = (row * sl1[rows, :]).astype(BF16)
                return carry

            each(tok, 16, slope_times)
        out = nt(gh1[pl.ds(start, count), :], w_in[1])
        if step < 5:
            pf[pl.ds(0, count), :] = out
            scatter_step(stg2, rcv2, step)
        else:
            pf2[...] = out

    ratio = -(sigma / alpha)
    sent(lats.at[pl.ds(0, (NZ - 1) * tok)], ag_send)
    for part, way in far_parts:
        scatter_end(stg2, rcv2, part)

        def back(at, carry):
            rows = pl.ds(part * size + at, 16)
            seen = imgs[pl.ds(own + part * size + at, 16), :].astype(F32)
            g_xn = pf2[rows, :] + (
                rcv2[0, 3, rows, :].astype(F32) + rcv2[1, 3, rows, :].astype(F32)
            )
            scale = lax.rsqrt(jnp.mean(seen * seen, axis=-1, keepdims=True) + EPS)
            weighted = gain1 * g_xn
            g_norm = scale * weighted - seen * (scale * scale * scale) * jnp.mean(
                seen * weighted, axis=-1, keepdims=True
            )
            g_images = (g_own + g_norm).astype(BF16).astype(F32)
            geps[pl.ds(own + part * size + at, 16), :] = (ratio * g_images).astype(BF16)
            return carry

        each(size, 16, back)
        gather_begin(geps, [(part, way)])

    gather_begin(geps, near_parts)

    def hidden_back(start, count):
        hp[pl.ds(0, count), :] = jnp.dot(
            geps[pl.ds(start, count), :], w_out[0], preferred_element_type=F32
        )

        def body(at, carry):
            rows = pl.ds(start + at, 16)
            gh0[rows, :] = (hp[pl.ds(at, 16), :] * sl0[rows, :]).astype(BF16)
            return carry

        each(count, 16, body)

    def weight_terms(a, start, count, first):
        left, right = ((geps, h0), (xn0, gh0))[a]
        rows = pl.ds(start, count)

        def body(i, carry):
            cols = pl.ds(pl.multiple_of(i * 256, 256), 256)
            term = tn(left[rows, cols], right[rows, :])
            if first:
                acc[a, cols, :] = term
            else:
                acc[a, cols, :] += term
            return carry

        lax.fori_loop(0, width // 256, body, None)

    def rows_of(a, slab, j, which):
        cx, cy = (slab, j) if a == 0 else (j, slab)
        return pl.ds(pl.multiple_of((cy // 2) * 640 + cx * 160 + (cy % 2) * 80 + which * 40, 40), 40)

    def pair(a, slab, part, which):
        return jnp.concatenate(
            [acc[a, rows_of(a, slab, 2 * part + j, which), :] for j in (0, 1)], axis=0
        )

    place = (x, y)
    along = (at_x, at_y)

    def core_copy(a, n):
        slab = (place[a] + (2, 1, 3, 0)[n]) % NR
        return remote(cstg.at[a, slab], crcv.at[a, slab], c_send, c_recv.at[a, n], partner)

    def early_terms():
        weight_terms(0, 4 * tok, 4 * tok, True)
        weight_terms(1, 4 * tok, 4 * tok, True)

    def slab_terms(a, n):
        slab = (place[a] + (2, 1, 3, 0)[n]) % NR
        if a == 0:
            blocks = [(s * 640 + slab * 160, 160) for s in (0, 1)]
        else:
            blocks = [((slab // 2) * 640 + cx * 160 + (slab % 2) * 80, 80) for cx in range(NR)]
        right = (h0, gh0)[a][pl.ds(0, 4 * tok), :]
        for start, count in blocks:
            rows = pl.ds(pl.multiple_of(start, 16), count)
            acc[a, rows, :] += jnp.dot(turned[a, rows, :], right, preferred_element_type=F32)
        for part in (0, 1):
            cstg[a, slab, pl.ds(80 * part, 80), :] = pair(a, slab, part, 1 - core).astype(BF16)
        core_copy(a, n).start()

    turned[1] = xn0[pl.ds(0, 4 * tok), :].T
    gather_with(geps, hidden_back, early_terms)
    gather_parts(geps, 4, far_parts)
    turned[0] = geps[pl.ds(0, 4 * tok), :].T
    slab_terms(0, 0)
    hidden_back(*arrived(4))
    for a, n in ((1, 0), (0, 1), (1, 1), (0, 2), (1, 2)):
        slab_terms(a, n)

    def own_part(a, distance, part):
        slab = (place[a] + distance) % NR
        return pair(a, slab, part, core) + crcv[a, slab, pl.ds(80 * part, 80), :].astype(F32)

    def ring_copy(a, way, step, part):
        at = (a, way, 2 * (step - 1) + part)
        rows = pl.ds(80 * part, 80)
        return remote(
            rstg.at[a, way, step - 1, rows], rrcv.at[a, way, step - 1, rows],
            g_send, g_recv.at[at], along[a](1 if way == 0 else -1),
        )

    def ring_send(a, way, step, part):
        distance = 2 if step == 1 else (1 if way == 0 else 3)
        value = own_part(a, distance, part)
        if step == 2 and part == way:
            ring_copy(a, way, 1, part).wait_recv()
            value = value + rrcv[a, way, 0, pl.ds(80 * part, 80), :].astype(F32)
        rstg[a, way, step - 1, pl.ds(80 * part, 80), :] = value.astype(BF16)
        ring_copy(a, way, step, part).start()

    for a in (0, 1):
        core_copy(a, 0).wait_recv()
        for way in (0, 1):
            ring_send(a, way, 1, way)
    for way in (0, 1):
        for a in (0, 1):
            core_copy(a, 1 + way).wait_recv()
            ring_send(a, way, 2, 1 - way)
    for a in (0, 1):
        slab_terms(a, 3)
    for a in (0, 1):
        for way in (0, 1):
            ring_send(a, way, 2, way)

    def last_copy(a, k):
        target = (place[1 - a] + k) % NR
        return remote(
            tstg.at[a, target], trcv.at[a, k - 1], t_send, t_recv.at[a, k - 1],
            along[1 - a](k),
        )

    for a in (0, 1):
        core_copy(a, 3).wait_recv()
        for part in (0, 1):
            value = own_part(a, 0, part)
            for way in (0, 1):
                ring_copy(a, way, 2, part).wait_recv()
                value = value + rrcv[a, way, 1, pl.ds(80 * part, 80), :].astype(F32)
            for j in (0, 1):
                rows = value[40 * j:40 * j + 40]
                tsum[a, 2 * part + j] = rows
                tstg[a, 2 * part + j] = jnp.concatenate(
                    [rows, jnp.zeros((8, hidden), F32)], axis=0
                ).astype(BF16)
        for k in range(1, NR):
            last_copy(a, k).start()
    for a, result in enumerate((gout, gin)):
        total = tsum[a, place[1 - a]]
        for k in range(1, NR):
            last_copy(a, k).wait_recv()
            total = total + trcv[a, k - 1].astype(F32)[:40]
        result[...] = total
    sent(lats.at[pl.ds(0, (NZ - 1) * tok)], ag_send)
    sent(lats.at[pl.ds(0, (NZ - 1) * tok)], rs_send)
    sent(w_in, w_send)
    sent(idb.at[pl.ds(0, NZ - 1)], id_send)
    sent(prcv, p_send)
    sent(prcv2, p2_send)
    sent(crcv, c_send)
    sent(w_in.at[0, pl.ds(0, 960)], g_send)
    sent(trcv, t_send)


def hand_over(left, right, left_out, right_out):
    left_out[...] = left[...]
    right_out[...] = right[...]


def on_device(latents, timesteps, prompt_ids, prompt_table, gains, w_in, w_out):
    tok, width = latents.shape[1:]
    hidden = w_in.shape[2]
    rows = NZ * tok
    vmem, dma = pltpu.VMEM, pltpu.SemaphoreType.DMA
    scratch = [
        vmem((2, width, hidden), BF16),
        vmem((2, width, hidden), BF16),
        vmem((rows, width), BF16),
        vmem((rows, width), BF16),
        vmem((rows, hidden), BF16),
        vmem((rows, hidden), F32),
        vmem((rows, width), BF16),
        vmem((rows, width), BF16),
        vmem((rows, hidden), F32),
        vmem((rows, hidden), BF16),
        vmem((rows, width), BF16),
        vmem((rows, hidden), BF16),
        vmem((2 * tok, hidden), F32),
        vmem((2 * tok, width), F32),
        vmem((tok, width), F32),
        vmem((2, 4, tok, width), BF16),
        vmem((2, 4, tok, width), BF16),
        vmem((2, 4, tok, width), BF16),
        vmem((2, 4, tok, width), BF16),
        vmem((NZ, 8, 128), jnp.int32),
        vmem((NZ, hidden), F32),
        vmem((NZ, width), F32),
        vmem((2 * NZ, width // 2), BF16),
        vmem((NZ - 1, 2 * NZ, width // 2), BF16),
        vmem((16, 128), BF16),
        vmem((NZ - 1, 16, 128), BF16),
        vmem((2, width, hidden), F32),
        vmem((2, width, rows // 2), BF16),
        vmem((2, NR, 160, hidden), BF16),
        vmem((2, NR, 160, hidden), BF16),
        vmem((2, 2, 2, 160, hidden), BF16),
        vmem((2, 2, 2, 160, hidden), BF16),
        vmem((2, NR, 48, hidden), BF16),
        vmem((2, NR, 40, hidden), F32),
        vmem((2, NR - 1, 48, hidden), BF16),
        dma((3,)),
        dma(()), dma((2, 8, 2)),
        dma(()), dma((2, 4 * PARTS)),
        dma(()), dma((2, 4 * PARTS)),
        dma(()), dma((7,)),
        dma(()), dma((7,)),
        dma(()), dma((7,)),
        dma(()), dma((2, 4)),
        dma(()), dma((2, 2, 4)),
        dma(()), dma((2, 3)),
    ]
    whole, scalar, away = (pl.BlockSpec(memory_space=s) for s in (pltpu.VMEM, pltpu.SMEM, pl.ANY))
    share = jax.ShapeDtypeStruct((width // 32, hidden), F32)
    shares = pl.pallas_call(
        kernel,
        out_shape=(share, share),
        in_specs=[away, scalar, scalar, whole, whole, away, away],
        out_specs=(whole, whole),
        scratch_shapes=scratch,
        compiler_params=pltpu.CompilerParams(
            collective_id=0, has_side_effects=True, vmem_limit_bytes=56 * 2**20
        ),
        name="draft_step",
    )(latents, timesteps, prompt_ids, prompt_table, gains, w_in, w_out)
    return pl.pallas_call(hand_over, out_shape=(share, share), name="hand_over")(*shares)


def solution(mesh):
    in_specs = (
        P(("dp", "tp"), None, None),
        P(("dp", "tp")),
        P(("dp", "tp")),
        P(),
        P(),
        P("sec", None, "tp"),
        P("sec", None, "tp"),
    )
    out_specs = (P(("sec", "dp"), "tp"), P(("sec", "dp"), "tp"))
    return jax.shard_map(
        on_device, mesh=mesh, in_specs=in_specs, out_specs=out_specs, check_vma=False
    )
```

```python
import functools
import math

import jax
import jax.numpy as jnp
from jax import lax
from jax.experimental import pallas as pl
from jax.experimental.pallas import tpu as pltpu
from jax.sharding import PartitionSpec as P

STEPS = 50
EPS = 1e-06
MESH = pl.DeviceIdType.MESH
F32, BF16 = jnp.float32, jnp.bfloat16

ORDER = (4, 5, 3, 6, 2, 7, 1, 0)
POS = {slot: pos for pos, slot in enumerate(ORDER)}
NZ, NR = 8, 4
FAR_FIRST = (4, 3, 5, 2, 6, 1, 7)
PARTS = 4


def gelu_and_slope(value):
    cdf = 0.5 * (1.0 + lax.erf(value * (1.0 / math.sqrt(2.0))))
    pdf = jnp.exp(-0.5 * value * value) * (1.0 / math.sqrt(2.0 * math.pi))
    return value * cdf, cdf + value * pdf


def nt(left, right):
    return lax.dot_general(left, right, (((1,), (1,)), ((), ())), preferred_element_type=F32)


def tn(left, right):
    return lax.dot_general(left, right, (((0,), (0,)), ((), ())), preferred_element_type=F32)


def kernel(
    lat, steps, ids, table, gains, win, wout, gin, gout,
    w_in, w_out, lats, xn0, h0, sl0, imgs, xn1, sl1, gh1, geps, gh0, hp, pf, pf2, stg1, rcv1, stg2,
    rcv2, idb, hm, pm, pmsg, prcv, pmsg2, prcv2, acc, turned, cstg, crcv, rstg, rrcv, tstg, tsum, trcv,
    local_sem, w_send, w_recv, ag_send, ag_recv, rs_send, rs_recv, id_send, id_recv, p_send, p_recv, p2_send, p2_recv,
    c_send, c_recv, g_send, g_recv, t_send, t_recv,
):
    tok, width = lat.shape[1], lat.shape[2]
    size = tok // PARTS
    hidden = win.shape[2]
    sec, dp, me = lax.axis_index("sec"), lax.axis_index("dp"), lax.axis_index("tp")
    x, ylo, core = dp // 4, (dp // 2) % 2, dp % 2
    y = sec * 2 + ylo
    other = 1 - sec

    def at_z(distance):
        return {"tp": (me + distance + NZ) % NZ}

    def at_x(distance):
        return {"dp": ((x + distance + NR) % NR) * 4 + ylo * 2 + core}

    def at_y(distance):
        there = (y + distance + NR) % NR
        return {"sec": there // 2, "dp": x * 4 + (there % 2) * 2 + core}

    partner = {"dp": x * 4 + ylo * 2 + (1 - core)}
    across = {"sec": other, "dp": x * 4 + (1 - ylo) * 2 + core}

    def remote(src, dst, send_sem, recv_sem, device):
        return pltpu.make_async_remote_copy(
            src_ref=src, dst_ref=dst, send_sem=send_sem, recv_sem=recv_sem,
            device_id=device, device_id_type=MESH,
        )

    def sent(ref, send_sem):
        remote(ref, ref, send_sem, c_recv.at[0, 0], partner).wait_send()

    here = [
        pltpu.make_async_copy(lat.at[sec], lats.at[pl.ds(POS[0] * tok, tok)], local_sem.at[0]),
        pltpu.make_async_copy(win.at[0], w_in.at[sec], local_sem.at[1]),
        pltpu.make_async_copy(wout.at[0], w_out.at[sec], local_sem.at[2]),
    ]
    for copy in here:
        copy.start()
    idb[0] = jnp.full((8, 128), ids[sec], jnp.int32)

    peers = [at(k) for at in (at_z, at_x, at_y) for k in (1, -1)] + [partner]
    barrier = pltpu.get_barrier_semaphore()
    for peer in peers:
        pl.semaphore_signal(barrier, inc=1, device_id=peer, device_id_type=MESH)
    pl.semaphore_wait(barrier, len(peers))

    def far(part, way):
        return part // (PARTS // 2) == way

    far_parts = [(p + way * (PARTS // 2), way) for p in range(PARTS // 2) for way in (0, 1)]
    near_parts = [(p + (1 - way) * (PARTS // 2), way) for p in range(PARTS // 2) for way in (0, 1)]

    def gather_copy(buf, way, step, part):
        if way == 0:
            src, dst, device = POS[step - 1], POS[step], at_z(1)
        else:
            src, dst, device = POS[(NZ - step + 1) % NZ], POS[NZ - step], at_z(-1)
        at = (way, PARTS * (step - 1) + part)
        return remote(
            buf.at[pl.ds(src * tok + part * size, size)],
            buf.at[pl.ds(dst * tok + part * size, size)],
            ag_send, ag_recv.at[at], device,
        )

    def gather_begin(buf, parts):
        for part, way in parts:
            gather_copy(buf, way, 1, part).start()

    def gather_parts(buf, step, parts):
        for part, way in parts:
            gather_copy(buf, way, step, part).wait_recv()
            if step + 1 < NZ // 2 or (step + 1 == NZ // 2 and far(part, way)):
                gather_copy(buf, way, step + 1, part).start()

    def gather_step(buf, step):
        gather_parts(buf, step, far_parts)
        if step < NZ // 2:
            gather_parts(buf, step, near_parts)

    def gather_with(buf, work, middle=None):
        work(*arrived(0))
        gather_step(buf, 1)
        for step in (1, 2, 3):
            start, count = arrived(step)
            work(start, tok)
            if step < 3:
                gather_parts(buf, step + 1, far_parts)
            work(start + tok, tok)
            if step == 2 and middle is not None:
                middle()
            if step < 3:
                gather_parts(buf, step + 1, near_parts)

    def arrived(step):
        if step == 0:
            return POS[0] * tok, tok
        if step == NZ // 2:
            return 0, tok
        return POS[NZ - step] * tok, 2 * tok

    def scatter_copy(stg, rcv, way, step, part):
        at = (way, PARTS * (step - 1) + part)
        rows = pl.ds(part * size, size)
        return remote(
            stg.at[way, step - 1, rows], rcv.at[way, step - 1, rows],
            rs_send, rs_recv.at[at], at_z(1) if way == 0 else at_z(-1),
        )

    def scatter_step(stg, rcv, step):
        for part, way in (near_parts if step > 1 else []) + far_parts:
            at = pl.ds(part * size, size)
            base = part * size + (way * tok if step > 1 else 0)
            value = pf[pl.ds(base, size), :]
            if step > 2 or (step == 2 and far(part, way)):
                scatter_copy(stg, rcv, way, step - 1, part).wait_recv()
                value = value + rcv[way, step - 2, at, :].astype(F32)
            stg[way, step - 1, at, :] = value.astype(BF16)
            scatter_copy(stg, rcv, way, step, part).start()

    def scatter_end(stg, rcv, part):
        for way in (0, 1):
            scatter_copy(stg, rcv, way, NZ // 2, part).wait_recv()

    def chunk(step):
        return arrived(5 - step) if step > 1 else (0, tok)

    quarter = (x + 2 * ylo) % NR

    def piece(offset, which, h):
        rows = (quarter + offset) % NR * (width // NR) + which * (width // NR // 2)
        return pl.ds(pl.multiple_of(rows + h * (width // NR // 4), 16), width // NR // 4)

    held = (w_in, w_out)
    given = (win, wout)
    beside = {"dp": x * 4 + (1 - ylo) * 2 + core}

    def weight_copy(a, kind, h):
        if kind == 0:
            rows = piece(2, core, h)
            src, dst, device = given[a].at[0, rows], held[a].at[sec, rows], across
        else:
            rows = piece((0, 0, 0, 0, 0, 3, 1, 2)[kind], core, h)
            src = dst = held[a].at[other, rows]
            device = (at_x(1), at_x(-1), beside, partner)[min(kind, 4) - 1]
        return remote(src, dst, w_send, w_recv.at[a, kind, h], device)

    def weight_landed(a, kind, h):
        ref = held[a].at[other, piece((0, 3, 1, 2)[kind % 4], core if kind < 4 else 1 - core, h)]
        remote(ref, ref, w_send, w_recv.at[a, kind, h], partner).wait_recv()

    def weights_first(a, h):
        weight_landed(a, 0, h)
        for kind in (1, 2, 3, 4):
            weight_copy(a, kind, h).start()

    def weights_second(a, h):
        for kind in (1, 2, 3):
            weight_landed(a, kind, h)
            weight_copy(a, kind + 4, h).start()

    def weights_last(a):
        for h in (0, 1):
            for kind in (4, 5, 6, 7):
                weight_landed(a, kind, h)

    def each(count, rows, body, init=None):
        return lax.fori_loop(0, count // rows, lambda i, c: body(pl.multiple_of(i * rows, rows), c), init)

    def norm(buf, dst, start, count, gain, slots=None):
        def body(at, total):
            value = buf[pl.ds(start + at, 16), :].astype(F32)
            scale = lax.rsqrt(jnp.mean(value * value, axis=-1, keepdims=True) + EPS)
            dst[pl.ds(start + at, 16), :] = (value * scale * gain).astype(BF16)
            return None if total is None else total + value[:8] + value[8:]

        if slots is None:
            each(count, 16, body)
            return
        for index, slot in enumerate(slots):
            start = POS[slot] * tok
            total = each(tok, 16, body, jnp.zeros((8, width), F32))
            pm[pl.ds(slot, 1), :] = jnp.sum(total, axis=0, keepdims=True) * (1.0 / tok)

    def slots_of(start, count):
        return ORDER[start // tok:(start + count) // tok]

    theta = (jnp.full((1, 128), steps[sec], jnp.int32).astype(F32) + 1.0) * (
        math.pi / 2.0 / (STEPS + 1.0)
    )
    alpha, sigma = jnp.cos(theta)[:, :1], jnp.sin(theta)[:, :1]
    for a in (0, 1):
        for h in (0, 1):
            weight_copy(a, 0, h).start()
    here[0].wait()
    gather_begin(lats, far_parts + near_parts)
    gain0, gain1 = gains[0:1, :], gains[1:2, :]
    norm(lats, xn0, *arrived(0), gain0)
    gather_step(lats, 1)
    weights_first(0, 0)
    norm(lats, xn0, *arrived(1), gain0)
    weights_first(0, 1)
    gather_step(lats, 2)
    weights_first(1, 0)
    weights_second(0, 0)
    norm(lats, xn0, *arrived(2), gain0)
    weights_first(1, 1)
    weights_second(0, 1)
    gather_step(lats, 3)
    weights_second(1, 0)
    norm(lats, xn0, *arrived(3), gain0)
    gather_step(lats, 4)
    weights_second(1, 1)
    for k in range(1, NZ):
        remote(idb.at[0], idb.at[k], id_send, id_recv.at[k - 1], at_z(k)).start()
    norm(lats, xn0, *arrived(4), gain0)
    here[1].wait()
    weights_last(0)

    def hidden0(start, count):
        hp[pl.ds(0, count), :] = jnp.dot(
            xn0[pl.ds(start, count), :], w_in[0], preferred_element_type=F32
        )

        def body(at, carry):
            act, slope = gelu_and_slope(hp[pl.ds(at, 16), :])
            h0[pl.ds(start + at, 16), :] = act.astype(BF16)
            sl0[pl.ds(start + at, 16), :] = slope
            return carry

        each(count, 16, body)

    hidden0(*chunk(1))
    here[2].wait()
    weights_last(1)

    for step in range(1, 6):
        start, count = chunk(step)
        if step > 1:
            hidden0(start, count)
        out = nt(h0[pl.ds(start, count), :], w_out[0])
        if step < 5:
            pf[pl.ds(0, count), :] = out
            scatter_step(stg1, rcv1, step)
        else:
            pf2[...] = out

    own = POS[0] * tok
    sent(lats.at[pl.ds(0, (NZ - 1) * tok)], ag_send)
    for part, way in far_parts:
        scatter_end(stg1, rcv1, part)

        def images(at, carry):
            rows = pl.ds(part * size + at, 16)
            base = lats[pl.ds(own + part * size + at, 16), :].astype(F32)
            mix = pf2[rows, :] + (rcv1[0, 3, rows, :].astype(F32) + rcv1[1, 3, rows, :].astype(F32))
            imgs[pl.ds(own + part * size + at, 16), :] = (
                (base - sigma * (base + mix)) / alpha
            ).astype(BF16)
            return carry

        each(size, 16, images)
        gather_begin(imgs, [(part, way)])

    gather_begin(imgs, near_parts)

    def hidden1(start, count):
        slots = slots_of(start, count)
        norm(imgs, xn1, start, count, gain1, slots)
        hp[pl.ds(0, count), :] = jnp.dot(
            xn1[pl.ds(start, count), :], w_in[1], preferred_element_type=F32
        )
        for index, slot in enumerate(slots):
            def body(at, total):
                act, slope = gelu_and_slope(hp[pl.ds(index * tok + at, 16), :])
                sl1[pl.ds(start + index * tok + at, 16), :] = slope
                act = act.astype(BF16).astype(F32)
                return total + act[:8] + act[8:]

            total = each(tok, 16, body, jnp.zeros((8, hidden), F32))
            hm[pl.ds(slot, 1), :] = jnp.sum(total, axis=0, keepdims=True) * (1.0 / tok)

    for k in range(1, NZ):
        remote(idb.at[k], idb.at[k], id_send, id_recv.at[k - 1], at_z(k)).wait_recv()
    id_rows = jnp.concatenate([idb[k, 0:1, :] for k in range(NZ)], axis=0)
    prompts = table.shape[0]
    onehot = (
        id_rows[:, :prompts] == lax.broadcasted_iota(jnp.int32, (NZ, prompts), 1)
    ).astype(F32).astype(BF16)
    text = jnp.dot(onehot, table[...], preferred_element_type=F32)
    text = text * lax.rsqrt(jnp.mean(text * text, axis=-1, keepdims=True) + EPS)
    def mixed_rows(rows):
        high = rows.astype(BF16).astype(F32)
        both = jnp.concatenate([high, rows - high], axis=0).astype(BF16)
        out = nt(both, w_out[1])
        return out[:NZ] + out[NZ:]

    def exchange(message, arrivals, send_sem, recv_sem, k):
        return remote(message, arrivals.at[k - 1], send_sem, recv_sem.at[k - 1], at_z(k))

    mid = width // 2
    opposite = NZ // 2
    hm[pl.ds(opposite, 1), :] = jnp.zeros((1, hidden), F32)
    gather_with(imgs, hidden1)
    mixed = mixed_rows(hm[...])
    pmsg[...] = jnp.concatenate([mixed[:, :mid], mixed[:, mid:]], axis=0).astype(BF16)
    for k in FAR_FIRST:
        exchange(pmsg, prcv, p_send, p_recv, k).start()
    gather_parts(imgs, 4, far_parts)
    hidden1(*arrived(4))

    lanes = width // 128
    last = mixed_rows(jnp.broadcast_to(hm[pl.ds(opposite, 1), :], (NZ, hidden)))[0:1]
    pmsg2[...] = jnp.concatenate(
        [last[:, 128 * i:128 * i + 128] for i in range(lanes)] + [jnp.zeros((16 - lanes, 128), F32)],
        axis=0,
    ).astype(BF16)
    for k in FAR_FIRST:
        exchange(pmsg2, prcv2, p2_send, p2_recv, k).start()
    pooled = pm[...] + mixed
    for k in range(1, NZ):
        exchange(pmsg, prcv, p_send, p_recv, k).wait_recv()
        got = prcv[k - 1].astype(F32)
        got = jnp.concatenate([got[:NZ], got[NZ:]], axis=1)
        pooled = pooled + jnp.concatenate([got[NZ - k:], got[:NZ - k]], axis=0)
    rows = {opposite: last}
    for k in range(1, NZ):
        exchange(pmsg2, prcv2, p2_send, p2_recv, k).wait_recv()
        got = prcv2[k - 1].astype(F32)
        rows[(opposite + k) % NZ] = jnp.concatenate([got[i:i + 1] for i in range(lanes)], axis=1)
    pooled = pooled + jnp.concatenate([rows[k] for k in range(NZ)], axis=0)
    unit = lax.rsqrt(jnp.mean(pooled * pooled, axis=-1, keepdims=True) + EPS)
    g_mean = (unit * text - pooled * (unit * unit * unit) * jnp.mean(
        pooled * text, axis=-1, keepdims=True
    )) * (-100.0 / width / tok)
    g_h1 = jnp.dot(g_mean.astype(BF16), w_out[1], preferred_element_type=F32)
    g_own = g_mean[0:1, :]
    sent(lats.at[pl.ds(0, (NZ - 1) * tok)], rs_send)

    for step in range(1, 6):
        start, count = chunk(step)
        for index, slot in enumerate(slots_of(start, count)):
            row = g_h1[slot:slot + 1, :]

            def slope_times(at, carry):
                rows = pl.ds(start + index * tok + at, 16)
                gh1[rows, :] = (row * sl1[rows, :]).astype(BF16)
                return carry

            each(tok, 16, slope_times)
        out = nt(gh1[pl.ds(start, count), :], w_in[1])
        if step < 5:
            pf[pl.ds(0, count), :] = out
            scatter_step(stg2, rcv2, step)
        else:
            pf2[...] = out

    ratio = -(sigma / alpha)
    sent(lats.at[pl.ds(0, (NZ - 1) * tok)], ag_send)
    for part, way in far_parts:
        scatter_end(stg2, rcv2, part)

        def back(at, carry):
            rows = pl.ds(part * size + at, 16)
            seen = imgs[pl.ds(own + part * size + at, 16), :].astype(F32)
            g_xn = pf2[rows, :] + (
                rcv2[0, 3, rows, :].astype(F32) + rcv2[1, 3, rows, :].astype(F32)
            )
            scale = lax.rsqrt(jnp.mean(seen * seen, axis=-1, keepdims=True) + EPS)
            weighted = gain1 * g_xn
            g_norm = scale * weighted - seen * (scale * scale * scale) * jnp.mean(
                seen * weighted, axis=-1, keepdims=True
            )
            g_images = (g_own + g_norm).astype(BF16).astype(F32)
            geps[pl.ds(own + part * size + at, 16), :] = (ratio * g_images).astype(BF16)
            return carry

        each(size, 16, back)
        gather_begin(geps, [(part, way)])

    gather_begin(geps, near_parts)

    def hidden_back(start, count):
        hp[pl.ds(0, count), :] = jnp.dot(
            geps[pl.ds(start, count), :], w_out[0], preferred_element_type=F32
        )

        def body(at, carry):
            rows = pl.ds(start + at, 16)
            gh0[rows, :] = (hp[pl.ds(at, 16), :] * sl0[rows, :]).astype(BF16)
            return carry

        each(count, 16, body)

    def weight_terms(a, start, count, first):
        left, right = ((geps, h0), (xn0, gh0))[a]
        rows = pl.ds(start, count)

        def body(i, carry):
            cols = pl.ds(pl.multiple_of(i * 256, 256), 256)
            term = tn(left[rows, cols], right[rows, :])
            if first:
                acc[a, cols, :] = term
            else:
                acc[a, cols, :] += term
            return carry

        lax.fori_loop(0, width // 256, body, None)

    def rows_of(a, slab, j, which):
        cx, cy = (slab, j) if a == 0 else (j, slab)
        return pl.ds(pl.multiple_of((cy // 2) * 640 + cx * 160 + (cy % 2) * 80 + which * 40, 40), 40)

    def pair(a, slab, part, which):
        return jnp.concatenate(
            [acc[a, rows_of(a, slab, 2 * part + j, which), :] for j in (0, 1)], axis=0
        )

    place = (x, y)
    along = (at_x, at_y)

    def core_copy(a, n):
        slab = (place[a] + (2, 1, 3, 0)[n]) % NR
        return remote(cstg.at[a, slab], crcv.at[a, slab], c_send, c_recv.at[a, n], partner)

    def early_terms():
        weight_terms(0, 4 * tok, 4 * tok, True)
        weight_terms(1, 4 * tok, 4 * tok, True)

    def slab_terms(a, n):
        slab = (place[a] + (2, 1, 3, 0)[n]) % NR
        if a == 0:
            blocks = [(s * 640 + slab * 160, 160) for s in (0, 1)]
        else:
            blocks = [((slab // 2) * 640 + cx * 160 + (slab % 2) * 80, 80) for cx in range(NR)]
        right = (h0, gh0)[a][pl.ds(0, 4 * tok), :]
        for start, count in blocks:
            rows = pl.ds(pl.multiple_of(start, 16), count)
            acc[a, rows, :] += jnp.dot(turned[a, rows, :], right, preferred_element_type=F32)
        for part in (0, 1):
            cstg[a, slab, pl.ds(80 * part, 80), :] = pair(a, slab, part, 1 - core).astype(BF16)
        core_copy(a, n).start()

    turned[1] = xn0[pl.ds(0, 4 * tok), :].T
    gather_with(geps, hidden_back, early_terms)
    gather_parts(geps, 4, far_parts)
    turned[0] = geps[pl.ds(0, 4 * tok), :].T
    slab_terms(0, 0)
    hidden_back(*arrived(4))
    for a, n in ((1, 0), (0, 1), (1, 1), (0, 2), (1, 2)):
        slab_terms(a, n)

    def own_part(a, distance, part):
        slab = (place[a] + distance) % NR
        return pair(a, slab, part, core) + crcv[a, slab, pl.ds(80 * part, 80), :].astype(F32)

    def ring_copy(a, way, step, part):
        at = (a, way, 2 * (step - 1) + part)
        rows = pl.ds(80 * part, 80)
        return remote(
            rstg.at[a, way, step - 1, rows], rrcv.at[a, way, step - 1, rows],
            g_send, g_recv.at[at], along[a](1 if way == 0 else -1),
        )

    def ring_send(a, way, step, part):
        distance = 2 if step == 1 else (1 if way == 0 else 3)
        value = own_part(a, distance, part)
        if step == 2 and part == way:
            ring_copy(a, way, 1, part).wait_recv()
            value = value + rrcv[a, way, 0, pl.ds(80 * part, 80), :].astype(F32)
        rstg[a, way, step - 1, pl.ds(80 * part, 80), :] = value.astype(BF16)
        ring_copy(a, way, step, part).start()

    for a in (0, 1):
        core_copy(a, 0).wait_recv()
        for way in (0, 1):
            ring_send(a, way, 1, way)
    for way in (0, 1):
        for a in (0, 1):
            core_copy(a, 1 + way).wait_recv()
            ring_send(a, way, 2, 1 - way)
    for a in (0, 1):
        slab_terms(a, 3)
    for a in (0, 1):
        for way in (0, 1):
            ring_send(a, way, 2, way)

    def last_copy(a, k):
        target = (place[1 - a] + k) % NR
        return remote(
            tstg.at[a, target], trcv.at[a, k - 1], t_send, t_recv.at[a, k - 1],
            along[1 - a](k),
        )

    for a in (0, 1):
        core_copy(a, 3).wait_recv()
        for part in (0, 1):
            value = own_part(a, 0, part)
            for way in (0, 1):
                ring_copy(a, way, 2, part).wait_recv()
                value = value + rrcv[a, way, 1, pl.ds(80 * part, 80), :].astype(F32)
            for j in (0, 1):
                rows = value[40 * j:40 * j + 40]
                tsum[a, 2 * part + j] = rows
                tstg[a, 2 * part + j] = jnp.concatenate(
                    [rows, jnp.zeros((8, hidden), F32)], axis=0
                ).astype(BF16)
        for k in (2, 1, 3):
            last_copy(a, k).start()
    for a, result in enumerate((gout, gin)):
        total = tsum[a, place[1 - a]]
        for k in range(1, NR):
            last_copy(a, k).wait_recv()
            total = total + trcv[a, k - 1].astype(F32)[:40]
        result[...] = total
    sent(lats.at[pl.ds(0, (NZ - 1) * tok)], ag_send)
    sent(lats.at[pl.ds(0, (NZ - 1) * tok)], rs_send)
    sent(w_in, w_send)
    sent(idb.at[pl.ds(0, NZ - 1)], id_send)
    sent(prcv, p_send)
    sent(prcv2, p2_send)
    sent(crcv, c_send)
    sent(w_in.at[0, pl.ds(0, 960)], g_send)
    sent(trcv, t_send)


def hand_over(left, right, left_out, right_out):
    left_out[...] = left[...]
    right_out[...] = right[...]


def on_device(latents, timesteps, prompt_ids, prompt_table, gains, w_in, w_out):
    tok, width = latents.shape[1:]
    hidden = w_in.shape[2]
    rows = NZ * tok
    vmem, dma = pltpu.VMEM, pltpu.SemaphoreType.DMA
    scratch = [
        vmem((2, width, hidden), BF16),
        vmem((2, width, hidden), BF16),
        vmem((rows, width), BF16),
        vmem((rows, width), BF16),
        vmem((rows, hidden), BF16),
        vmem((rows, hidden), F32),
        vmem((rows, width), BF16),
        vmem((rows, width), BF16),
        vmem((rows, hidden), F32),
        vmem((rows, hidden), BF16),
        vmem((rows, width), BF16),
        vmem((rows, hidden), BF16),
        vmem((2 * tok, hidden), F32),
        vmem((2 * tok, width), F32),
        vmem((tok, width), F32),
        vmem((2, 4, tok, width), BF16),
        vmem((2, 4, tok, width), BF16),
        vmem((2, 4, tok, width), BF16),
        vmem((2, 4, tok, width), BF16),
        vmem((NZ, 8, 128), jnp.int32),
        vmem((NZ, hidden), F32),
        vmem((NZ, width), F32),
        vmem((2 * NZ, width // 2), BF16),
        vmem((NZ - 1, 2 * NZ, width // 2), BF16),
        vmem((16, 128), BF16),
        vmem((NZ - 1, 16, 128), BF16),
        vmem((2, width, hidden), F32),
        vmem((2, width, rows // 2), BF16),
        vmem((2, NR, 160, hidden), BF16),
        vmem((2, NR, 160, hidden), BF16),
        vmem((2, 2, 2, 160, hidden), BF16),
        vmem((2, 2, 2, 160, hidden), BF16),
        vmem((2, NR, 48, hidden), BF16),
        vmem((2, NR, 40, hidden), F32),
        vmem((2, NR - 1, 48, hidden), BF16),
        dma((3,)),
        dma(()), dma((2, 8, 2)),
        dma(()), dma((2, 4 * PARTS)),
        dma(()), dma((2, 4 * PARTS)),
        dma(()), dma((7,)),
        dma(()), dma((7,)),
        dma(()), dma((7,)),
        dma(()), dma((2, 4)),
        dma(()), dma((2, 2, 4)),
        dma(()), dma((2, 3)),
    ]
    whole, scalar, away = (pl.BlockSpec(memory_space=s) for s in (pltpu.VMEM, pltpu.SMEM, pl.ANY))
    share = jax.ShapeDtypeStruct((width // 32, hidden), F32)
    shares = pl.pallas_call(
        kernel,
        out_shape=(share, share),
        in_specs=[away, scalar, scalar, whole, whole, away, away],
        out_specs=(whole, whole),
        scratch_shapes=scratch,
        compiler_params=pltpu.CompilerParams(
            collective_id=0, has_side_effects=True, vmem_limit_bytes=56 * 2**20
        ),
        name="draft_step",
    )(latents, timesteps, prompt_ids, prompt_table, gains, w_in, w_out)
    return pl.pallas_call(hand_over, out_shape=(share, share), name="hand_over")(*shares)


def solution(mesh):
    in_specs = (
        P(("dp", "tp"), None, None),
        P(("dp", "tp")),
        P(("dp", "tp")),
        P(),
        P(),
        P("sec", None, "tp"),
        P("sec", None, "tp"),
    )
    out_specs = (P(("sec", "dp"), "tp"), P(("sec", "dp"), "tp"))
    return jax.shard_map(
        on_device, mesh=mesh, in_specs=in_specs, out_specs=out_specs, check_vma=False
    )
```

```python
import functools
import math

import jax
import jax.numpy as jnp
from jax import lax
from jax.experimental import pallas as pl
from jax.experimental.pallas import tpu as pltpu
from jax.sharding import PartitionSpec as P

STEPS = 50
EPS = 1e-06
MESH = pl.DeviceIdType.MESH
F32, BF16 = jnp.float32, jnp.bfloat16

ORDER = (4, 5, 3, 6, 2, 7, 1, 0)
POS = {slot: pos for pos, slot in enumerate(ORDER)}
NZ, NR = 8, 4
FAR_FIRST = (4, 3, 5, 2, 6, 1, 7)
PARTS = 4


def gelu_and_slope(value):
    cdf = 0.5 * (1.0 + lax.erf(value * (1.0 / math.sqrt(2.0))))
    pdf = jnp.exp(-0.5 * value * value) * (1.0 / math.sqrt(2.0 * math.pi))
    return value * cdf, cdf + value * pdf


def nt(left, right):
    return lax.dot_general(left, right, (((1,), (1,)), ((), ())), preferred_element_type=F32)


def tn(left, right):
    return lax.dot_general(left, right, (((0,), (0,)), ((), ())), preferred_element_type=F32)


def kernel(
    lat, steps, ids, table, gains, win, wout, gin, gout,
    w_in, w_out, lats, xn0, h0, sl0, imgs, xn1, sl1, gh1, geps, gh0, hp, pf, pf2, stg1, rcv1, stg2,
    rcv2, idb, hm, pm, pmsg, prcv, pmsg2, prcv2, acc, turned, cstg, crcv, rstg, rrcv, tstg, tsum, trcv,
    local_sem, w_send, w_recv, ag_send, ag_recv, rs_send, rs_recv, id_send, id_recv, p_send, p_recv, p2_send, p2_recv,
    c_send, c_recv, g_send, g_recv, t_send, t_recv,
):
    tok, width = lat.shape[1], lat.shape[2]
    size = tok // PARTS
    hidden = win.shape[2]
    sec, dp, me = lax.axis_index("sec"), lax.axis_index("dp"), lax.axis_index("tp")
    x, ylo, core = dp // 4, (dp // 2) % 2, dp % 2
    y = sec * 2 + ylo
    other = 1 - sec

    def at_z(distance):
        return {"tp": (me + distance + NZ) % NZ}

    def at_x(distance):
        return {"dp": ((x + distance + NR) % NR) * 4 + ylo * 2 + core}

    def at_y(distance):
        there = (y + distance + NR) % NR
        return {"sec": there // 2, "dp": x * 4 + (there % 2) * 2 + core}

    partner = {"dp": x * 4 + ylo * 2 + (1 - core)}
    across = {"sec": other, "dp": x * 4 + (1 - ylo) * 2 + core}

    def remote(src, dst, send_sem, recv_sem, device):
        return pltpu.make_async_remote_copy(
            src_ref=src, dst_ref=dst, send_sem=send_sem, recv_sem=recv_sem,
            device_id=device, device_id_type=MESH,
        )

    def sent(ref, send_sem):
        remote(ref, ref, send_sem, c_recv.at[0, 0], partner).wait_send()

    here = [
        pltpu.make_async_copy(lat.at[sec], lats.at[pl.ds(POS[0] * tok, tok)], local_sem.at[0]),
        pltpu.make_async_copy(win.at[0], w_in.at[sec], local_sem.at[1]),
        pltpu.make_async_copy(wout.at[0], w_out.at[sec], local_sem.at[2]),
    ]
    for copy in here:
        copy.start()
    idb[0] = jnp.full((8, 128), ids[sec], jnp.int32)

    peers = [at(k) for at in (at_z, at_x, at_y) for k in (1, -1)] + [partner]
    barrier = pltpu.get_barrier_semaphore()
    for peer in peers:
        pl.semaphore_signal(barrier, inc=1, device_id=peer, device_id_type=MESH)
    pl.semaphore_wait(barrier, len(peers))

    def far(part, way):
        return part // (PARTS // 2) == way

    far_parts = [(p + way * (PARTS // 2), way) for p in range(PARTS // 2) for way in (0, 1)]
    near_parts = [(p + (1 - way) * (PARTS // 2), way) for p in range(PARTS // 2) for way in (0, 1)]

    def gather_copy(buf, way, step, part):
        if way == 0:
            src, dst, device = POS[step - 1], POS[step], at_z(1)
        else:
            src, dst, device = POS[(NZ - step + 1) % NZ], POS[NZ - step], at_z(-1)
        at = (way, PARTS * (step - 1) + part)
        return remote(
            buf.at[pl.ds(src * tok + part * size, size)],
            buf.at[pl.ds(dst * tok + part * size, size)],
            ag_send, ag_recv.at[at], device,
        )

    def gather_begin(buf, parts):
        for part, way in parts:
            gather_copy(buf, way, 1, part).start()

    def gather_parts(buf, step, parts):
        for part, way in parts:
            gather_copy(buf, way, step, part).wait_recv()
            if step + 1 < NZ // 2 or (step + 1 == NZ // 2 and far(part, way)):
                gather_copy(buf, way, step + 1, part).start()

    def gather_step(buf, step):
        gather_parts(buf, step, far_parts)
        if step < NZ // 2:
            gather_parts(buf, step, near_parts)

    def gather_with(buf, work, middle=None):
        work(*arrived(0))
        gather_step(buf, 1)
        for step in (1, 2, 3):
            start, count = arrived(step)
            work(start, tok)
            if step < 3:
                gather_parts(buf, step + 1, far_parts)
            work(start + tok, tok)
            if step == 2 and middle is not None:
                middle()
            if step < 3:
                gather_parts(buf, step + 1, near_parts)

    def arrived(step):
        if step == 0:
            return POS[0] * tok, tok
        if step == NZ // 2:
            return 0, tok
        return POS[NZ - step] * tok, 2 * tok

    def scatter_copy(stg, rcv, way, step, part):
        at = (way, PARTS * (step - 1) + part)
        rows = pl.ds(part * size, size)
        return remote(
            stg.at[way, step - 1, rows], rcv.at[way, step - 1, rows],
            rs_send, rs_recv.at[at], at_z(1) if way == 0 else at_z(-1),
        )

    def scatter_step(stg, rcv, step):
        for part, way in (near_parts if step > 1 else []) + far_parts:
            at = pl.ds(part * size, size)
            base = part * size + (way * tok if step > 1 else 0)
            value = pf[pl.ds(base, size), :]
            if step > 2 or (step == 2 and far(part, way)):
                scatter_copy(stg, rcv, way, step - 1, part).wait_recv()
                value = value + rcv[way, step - 2, at, :].astype(F32)
            stg[way, step - 1, at, :] = value.astype(BF16)
            scatter_copy(stg, rcv, way, step, part).start()

    def scatter_end(stg, rcv, part):
        for way in (0, 1):
            scatter_copy(stg, rcv, way, NZ // 2, part).wait_recv()

    def chunk(step):
        return arrived(5 - step) if step > 1 else (0, tok)

    quarter = (x + 2 * ylo) % NR

    def piece(offset, which, h):
        rows = (quarter + offset) % NR * (width // NR) + which * (width // NR // 2)
        return pl.ds(pl.multiple_of(rows + h * (width // NR // 4), 16), width // NR // 4)

    held = (w_in, w_out)
    given = (win, wout)
    beside = {"dp": x * 4 + (1 - ylo) * 2 + core}

    def weight_copy(a, kind, h):
        if kind == 0:
            rows = piece(2, core, h)
            src, dst, device = given[a].at[0, rows], held[a].at[sec, rows], across
        else:
            rows = piece((0, 0, 0, 0, 0, 3, 1, 2)[kind], core, h)
            src = dst = held[a].at[other, rows]
            device = (at_x(1), at_x(-1), beside, partner)[min(kind, 4) - 1]
        return remote(src, dst, w_send, w_recv.at[a, kind, h], device)

    def weight_landed(a, kind, h):
        ref = held[a].at[other, piece((0, 3, 1, 2)[kind % 4], core if kind < 4 else 1 - core, h)]
        remote(ref, ref, w_send, w_recv.at[a, kind, h], partner).wait_recv()

    def weights_first(a, h):
        weight_landed(a, 0, h)
        for kind in (1, 2, 3, 4):
            weight_copy(a, kind, h).start()

    def weights_second(a, h):
        for kind in (1, 2, 3):
            weight_landed(a, kind, h)
            weight_copy(a, kind + 4, h).start()

    def weights_last(a):
        for h in (0, 1):
            for kind in (4, 5, 6, 7):
                weight_landed(a, kind, h)

    def each(count, rows, body, init=None):
        several = min(4, count // rows)

        def group(i, carry):
            for j in range(several):
                carry = body(pl.multiple_of((i * several + j) * rows, rows), carry)
            return carry

        return lax.fori_loop(0, count // rows // several, group, init)

    def norm(buf, dst, start, count, gain, slots=None):
        def body(at, total):
            value = buf[pl.ds(start + at, 16), :].astype(F32)
            scale = lax.rsqrt(jnp.mean(value * value, axis=-1, keepdims=True) + EPS)
            dst[pl.ds(start + at, 16), :] = (value * scale * gain).astype(BF16)
            return None if total is None else total + value[:8] + value[8:]

        if slots is None:
            each(count, 16, body)
            return
        for index, slot in enumerate(slots):
            start = POS[slot] * tok
            total = each(tok, 16, body, jnp.zeros((8, width), F32))
            pm[pl.ds(slot, 1), :] = jnp.sum(total, axis=0, keepdims=True) * (1.0 / tok)

    def slots_of(start, count):
        return ORDER[start // tok:(start + count) // tok]

    theta = (jnp.full((1, 128), steps[sec], jnp.int32).astype(F32) + 1.0) * (
        math.pi / 2.0 / (STEPS + 1.0)
    )
    alpha, sigma = jnp.cos(theta)[:, :1], jnp.sin(theta)[:, :1]
    for a in (0, 1):
        for h in (0, 1):
            weight_copy(a, 0, h).start()
    here[0].wait()
    gather_begin(lats, far_parts + near_parts)
    gain0, gain1 = gains[0:1, :], gains[1:2, :]
    norm(lats, xn0, *arrived(0), gain0)
    gather_step(lats, 1)
    weights_first(0, 0)
    norm(lats, xn0, *arrived(1), gain0)
    weights_first(0, 1)
    gather_step(lats, 2)
    weights_first(1, 0)
    weights_second(0, 0)
    norm(lats, xn0, *arrived(2), gain0)
    weights_first(1, 1)
    weights_second(0, 1)
    gather_step(lats, 3)
    weights_second(1, 0)
    norm(lats, xn0, *arrived(3), gain0)
    gather_step(lats, 4)
    weights_second(1, 1)
    for k in range(1, NZ):
        remote(idb.at[0], idb.at[k], id_send, id_recv.at[k - 1], at_z(k)).start()
    norm(lats, xn0, *arrived(4), gain0)
    here[1].wait()
    weights_last(0)

    def hidden0(start, count):
        hp[pl.ds(0, count), :] = jnp.dot(
            xn0[pl.ds(start, count), :], w_in[0], preferred_element_type=F32
        )

        def body(at, carry):
            act, slope = gelu_and_slope(hp[pl.ds(at, 16), :])
            h0[pl.ds(start + at, 16), :] = act.astype(BF16)
            sl0[pl.ds(start + at, 16), :] = slope
            return carry

        each(count, 16, body)

    hidden0(*chunk(1))
    here[2].wait()
    weights_last(1)

    for step in range(1, 6):
        start, count = chunk(step)
        if step > 1:
            hidden0(start, count)
        out = nt(h0[pl.ds(start, count), :], w_out[0])
        if step < 5:
            pf[pl.ds(0, count), :] = out
            scatter_step(stg1, rcv1, step)
        else:
            pf2[...] = out

    own = POS[0] * tok
    sent(lats.at[pl.ds(0, (NZ - 1) * tok)], ag_send)
    for part, way in far_parts:
        scatter_end(stg1, rcv1, part)

        def images(at, carry):
            rows = pl.ds(part * size + at, 16)
            base = lats[pl.ds(own + part * size + at, 16), :].astype(F32)
            mix = pf2[rows, :] + (rcv1[0, 3, rows, :].astype(F32) + rcv1[1, 3, rows, :].astype(F32))
            imgs[pl.ds(own + part * size + at, 16), :] = (
                (base - sigma * (base + mix)) / alpha
            ).astype(BF16)
            return carry

        each(size, 16, images)
        gather_begin(imgs, [(part, way)])

    gather_begin(imgs, near_parts)

    def hidden1(start, count):
        slots = slots_of(start, count)
        norm(imgs, xn1, start, count, gain1, slots)
        hp[pl.ds(0, count), :] = jnp.dot(
            xn1[pl.ds(start, count), :], w_in[1], preferred_element_type=F32
        )
        for index, slot in enumerate(slots):
            def body(at, total):
                act, slope = gelu_and_slope(hp[pl.ds(index * tok + at, 16), :])
                sl1[pl.ds(start + index * tok + at, 16), :] = slope
                act = act.astype(BF16).astype(F32)
                return total + act[:8] + act[8:]

            total = each(tok, 16, body, jnp.zeros((8, hidden), F32))
            hm[pl.ds(slot, 1), :] = jnp.sum(total, axis=0, keepdims=True) * (1.0 / tok)

    for k in range(1, NZ):
        remote(idb.at[k], idb.at[k], id_send, id_recv.at[k - 1], at_z(k)).wait_recv()
    id_rows = jnp.concatenate([idb[k, 0:1, :] for k in range(NZ)], axis=0)
    prompts = table.shape[0]
    onehot = (
        id_rows[:, :prompts] == lax.broadcasted_iota(jnp.int32, (NZ, prompts), 1)
    ).astype(F32).astype(BF16)
    text = jnp.dot(onehot, table[...], preferred_element_type=F32)
    text = text * lax.rsqrt(jnp.mean(text * text, axis=-1, keepdims=True) + EPS)
    def mixed_rows(rows):
        high = rows.astype(BF16).astype(F32)
        both = jnp.concatenate([high, rows - high], axis=0).astype(BF16)
        out = nt(both, w_out[1])
        return out[:NZ] + out[NZ:]

    def exchange(message, arrivals, send_sem, recv_sem, k):
        return remote(message, arrivals.at[k - 1], send_sem, recv_sem.at[k - 1], at_z(k))

    mid = width // 2
    opposite = NZ // 2
    hm[pl.ds(opposite, 1), :] = jnp.zeros((1, hidden), F32)
    gather_with(imgs, hidden1)
    mixed = mixed_rows(hm[...])
    pmsg[...] = jnp.concatenate([mixed[:, :mid], mixed[:, mid:]], axis=0).astype(BF16)
    for k in FAR_FIRST:
        exchange(pmsg, prcv, p_send, p_recv, k).start()
    gather_parts(imgs, 4, far_parts)
    hidden1(*arrived(4))

    lanes = width // 128
    last = mixed_rows(jnp.broadcast_to(hm[pl.ds(opposite, 1), :], (NZ, hidden)))[0:1]
    pmsg2[...] = jnp.concatenate(
        [last[:, 128 * i:128 * i + 128] for i in range(lanes)] + [jnp.zeros((16 - lanes, 128), F32)],
        axis=0,
    ).astype(BF16)
    for k in FAR_FIRST:
        exchange(pmsg2, prcv2, p2_send, p2_recv, k).start()
    pooled = pm[...] + mixed
    for k in range(1, NZ):
        exchange(pmsg, prcv, p_send, p_recv, k).wait_recv()
        got = prcv[k - 1].astype(F32)
        got = jnp.concatenate([got[:NZ], got[NZ:]], axis=1)
        pooled = pooled + jnp.concatenate([got[NZ - k:], got[:NZ - k]], axis=0)
    rows = {opposite: last}
    for k in range(1, NZ):
        exchange(pmsg2, prcv2, p2_send, p2_recv, k).wait_recv()
        got = prcv2[k - 1].astype(F32)
        rows[(opposite + k) % NZ] = jnp.concatenate([got[i:i + 1] for i in range(lanes)], axis=1)
    pooled = pooled + jnp.concatenate([rows[k] for k in range(NZ)], axis=0)
    unit = lax.rsqrt(jnp.mean(pooled * pooled, axis=-1, keepdims=True) + EPS)
    g_mean = (unit * text - pooled * (unit * unit * unit) * jnp.mean(
        pooled * text, axis=-1, keepdims=True
    )) * (-100.0 / width / tok)
    g_h1 = jnp.dot(g_mean.astype(BF16), w_out[1], preferred_element_type=F32)
    g_own = g_mean[0:1, :]
    sent(lats.at[pl.ds(0, (NZ - 1) * tok)], rs_send)

    for step in range(1, 6):
        start, count = chunk(step)
        for index, slot in enumerate(slots_of(start, count)):
            row = g_h1[slot:slot + 1, :]

            def slope_times(at, carry):
                rows = pl.ds(start + index * tok + at, 16)
                gh1[rows, :] = (row * sl1[rows, :]).astype(BF16)
                return carry

            each(tok, 16, slope_times)
        out = nt(gh1[pl.ds(start, count), :], w_in[1])
        if step < 5:
            pf[pl.ds(0, count), :] = out
            scatter_step(stg2, rcv2, step)
        else:
            pf2[...] = out

    ratio = -(sigma / alpha)
    sent(lats.at[pl.ds(0, (NZ - 1) * tok)], ag_send)
    for part, way in far_parts:
        scatter_end(stg2, rcv2, part)

        def back(at, carry):
            rows = pl.ds(part * size + at, 16)
            seen = imgs[pl.ds(own + part * size + at, 16), :].astype(F32)
            g_xn = pf2[rows, :] + (
                rcv2[0, 3, rows, :].astype(F32) + rcv2[1, 3, rows, :].astype(F32)
            )
            scale = lax.rsqrt(jnp.mean(seen * seen, axis=-1, keepdims=True) + EPS)
            weighted = gain1 * g_xn
            g_norm = scale * weighted - seen * (scale * scale * scale) * jnp.mean(
                seen * weighted, axis=-1, keepdims=True
            )
            g_images = (g_own + g_norm).astype(BF16).astype(F32)
            geps[pl.ds(own + part * size + at, 16), :] = (ratio * g_images).astype(BF16)
            return carry

        each(size, 16, back)
        gather_begin(geps, [(part, way)])

    gather_begin(geps, near_parts)

    def hidden_back(start, count):
        hp[pl.ds(0, count), :] = jnp.dot(
            geps[pl.ds(start, count), :], w_out[0], preferred_element_type=F32
        )

        def body(at, carry):
            rows = pl.ds(start + at, 16)
            gh0[rows, :] = (hp[pl.ds(at, 16), :] * sl0[rows, :]).astype(BF16)
            return carry

        each(count, 16, body)

    def weight_terms(a, start, count):
        left, right = ((geps, h0), (xn0, gh0))[a]
        rows = pl.ds(start, count)

        for i in range(width // 256):
            cols = pl.ds(i * 256, 256)
            acc[a, cols, :] = tn(left[rows, cols], right[rows, :])

    def rows_of(a, slab, j, which):
        cx, cy = (slab, j) if a == 0 else (j, slab)
        return pl.ds(pl.multiple_of((cy // 2) * 640 + cx * 160 + (cy % 2) * 80 + which * 40, 40), 40)

    def pair(a, slab, part, which):
        return jnp.concatenate(
            [acc[a, rows_of(a, slab, 2 * part + j, which), :] for j in (0, 1)], axis=0
        )

    place = (x, y)
    along = (at_x, at_y)

    def core_copy(a, n):
        slab = (place[a] + (2, 1, 3, 0)[n]) % NR
        return remote(cstg.at[a, slab], crcv.at[a, slab], c_send, c_recv.at[a, n], partner)

    def early_terms():
        weight_terms(0, 4 * tok, 4 * tok)
        weight_terms(1, 4 * tok, 4 * tok)

    def slab_terms(a, n):
        slab = (place[a] + (2, 1, 3, 0)[n]) % NR
        if a == 0:
            blocks = [(s * 640 + slab * 160, 160) for s in (0, 1)]
        else:
            blocks = [((slab // 2) * 640 + cx * 160 + (slab % 2) * 80, 80) for cx in range(NR)]
        right = (h0, gh0)[a][pl.ds(0, 4 * tok), :]
        for start, count in blocks:
            rows = pl.ds(pl.multiple_of(start, 16), count)
            acc[a, rows, :] += jnp.dot(turned[a, rows, :], right, preferred_element_type=F32)
        for part in (0, 1):
            cstg[a, slab, pl.ds(80 * part, 80), :] = pair(a, slab, part, 1 - core).astype(BF16)
        core_copy(a, n).start()

    turned[1] = xn0[pl.ds(0, 4 * tok), :].T
    gather_with(geps, hidden_back, early_terms)
    gather_parts(geps, 4, far_parts)
    turned[0] = geps[pl.ds(0, 4 * tok), :].T
    slab_terms(0, 0)
    hidden_back(*arrived(4))
    for a, n in ((1, 0), (0, 1), (1, 1), (0, 2), (1, 2)):
        slab_terms(a, n)

    def own_part(a, distance, part):
        slab = (place[a] + distance) % NR
        return pair(a, slab, part, core) + crcv[a, slab, pl.ds(80 * part, 80), :].astype(F32)

    def ring_copy(a, way, step, part):
        at = (a, way, 2 * (step - 1) + part)
        rows = pl.ds(80 * part, 80)
        return remote(
            rstg.at[a, way, step - 1, rows], rrcv.at[a, way, step - 1, rows],
            g_send, g_recv.at[at], along[a](1 if way == 0 else -1),
        )

    def ring_send(a, way, step, part):
        distance = 2 if step == 1 else (1 if way == 0 else 3)
        value = own_part(a, distance, part)
        if step == 2 and part == way:
            ring_copy(a, way, 1, part).wait_recv()
            value = value + rrcv[a, way, 0, pl.ds(80 * part, 80), :].astype(F32)
        rstg[a, way, step - 1, pl.ds(80 * part, 80), :] = value.astype(BF16)
        ring_copy(a, way, step, part).start()

    for a in (0, 1):
        core_copy(a, 0).wait_recv()
        for way in (0, 1):
            ring_send(a, way, 1, way)
    for way in (0, 1):
        for a in (0, 1):
            core_copy(a, 1 + way).wait_recv()
            ring_send(a, way, 2, 1 - way)
    for a in (0, 1):
        slab_terms(a, 3)
    for a in (0, 1):
        for way in (0, 1):
            ring_send(a, way, 2, way)

    def last_copy(a, k):
        target = (place[1 - a] + k) % NR
        return remote(
            tstg.at[a, target], trcv.at[a, k - 1], t_send, t_recv.at[a, k - 1],
            along[1 - a](k),
        )

    for a in (0, 1):
        core_copy(a, 3).wait_recv()
        for part in (0, 1):
            value = own_part(a, 0, part)
            for way in (0, 1):
                ring_copy(a, way, 2, part).wait_recv()
                value = value + rrcv[a, way, 1, pl.ds(80 * part, 80), :].astype(F32)
            for j in (0, 1):
                rows = value[40 * j:40 * j + 40]
                tsum[a, 2 * part + j] = rows
                tstg[a, 2 * part + j] = jnp.concatenate(
                    [rows, jnp.zeros((8, hidden), F32)], axis=0
                ).astype(BF16)
        for k in (2, 1, 3):
            last_copy(a, k).start()
    for a, result in enumerate((gout, gin)):
        total = tsum[a, place[1 - a]]
        for k in range(1, NR):
            last_copy(a, k).wait_recv()
            total = total + trcv[a, k - 1].astype(F32)[:40]
        result[...] = total
    sent(lats.at[pl.ds(0, (NZ - 1) * tok)], ag_send)
    sent(lats.at[pl.ds(0, (NZ - 1) * tok)], rs_send)
    sent(w_in, w_send)
    sent(idb.at[pl.ds(0, NZ - 1)], id_send)
    sent(prcv, p_send)
    sent(prcv2, p2_send)
    sent(crcv, c_send)
    sent(w_in.at[0, pl.ds(0, 960)], g_send)
    sent(trcv, t_send)


def hand_over(left, right, left_out, right_out):
    left_out[...] = left[...]
    right_out[...] = right[...]


def on_device(latents, timesteps, prompt_ids, prompt_table, gains, w_in, w_out):
    tok, width = latents.shape[1:]
    hidden = w_in.shape[2]
    rows = NZ * tok
    vmem, dma = pltpu.VMEM, pltpu.SemaphoreType.DMA
    scratch = [
        vmem((2, width, hidden), BF16),
        vmem((2, width, hidden), BF16),
        vmem((rows, width), BF16),
        vmem((rows, width), BF16),
        vmem((rows, hidden), BF16),
        vmem((rows, hidden), F32),
        vmem((rows, width), BF16),
        vmem((rows, width), BF16),
        vmem((rows, hidden), F32),
        vmem((rows, hidden), BF16),
        vmem((rows, width), BF16),
        vmem((rows, hidden), BF16),
        vmem((2 * tok, hidden), F32),
        vmem((2 * tok, width), F32),
        vmem((tok, width), F32),
        vmem((2, 4, tok, width), BF16),
        vmem((2, 4, tok, width), BF16),
        vmem((2, 4, tok, width), BF16),
        vmem((2, 4, tok, width), BF16),
        vmem((NZ, 8, 128), jnp.int32),
        vmem((NZ, hidden), F32),
        vmem((NZ, width), F32),
        vmem((2 * NZ, width // 2), BF16),
        vmem((NZ - 1, 2 * NZ, width // 2), BF16),
        vmem((16, 128), BF16),
        vmem((NZ - 1, 16, 128), BF16),
        vmem((2, width, hidden), F32),
        vmem((2, width, rows // 2), BF16),
        vmem((2, NR, 160, hidden), BF16),
        vmem((2, NR, 160, hidden), BF16),
        vmem((2, 2, 2, 160, hidden), BF16),
        vmem((2, 2, 2, 160, hidden), BF16),
        vmem((2, NR, 48, hidden), BF16),
        vmem((2, NR, 40, hidden), F32),
        vmem((2, NR - 1, 48, hidden), BF16),
        dma((3,)),
        dma(()), dma((2, 8, 2)),
        dma(()), dma((2, 4 * PARTS)),
        dma(()), dma((2, 4 * PARTS)),
        dma(()), dma((7,)),
        dma(()), dma((7,)),
        dma(()), dma((7,)),
        dma(()), dma((2, 4)),
        dma(()), dma((2, 2, 4)),
        dma(()), dma((2, 3)),
    ]
    whole, scalar, away = (pl.BlockSpec(memory_space=s) for s in (pltpu.VMEM, pltpu.SMEM, pl.ANY))
    share = jax.ShapeDtypeStruct((width // 32, hidden), F32)
    shares = pl.pallas_call(
        kernel,
        out_shape=(share, share),
        in_specs=[away, scalar, scalar, whole, whole, away, away],
        out_specs=(whole, whole),
        scratch_shapes=scratch,
        compiler_params=pltpu.CompilerParams(
            collective_id=0, has_side_effects=True, vmem_limit_bytes=56 * 2**20
        ),
        name="draft_step",
    )(latents, timesteps, prompt_ids, prompt_table, gains, w_in, w_out)
    return pl.pallas_call(hand_over, out_shape=(share, share), name="hand_over")(*shares)


def solution(mesh):
    in_specs = (
        P(("dp", "tp"), None, None),
        P(("dp", "tp")),
        P(("dp", "tp")),
        P(),
        P(),
        P("sec", None, "tp"),
        P("sec", None, "tp"),
    )
    out_specs = (P(("sec", "dp"), "tp"), P(("sec", "dp"), "tp"))
    return jax.shard_map(
        on_device, mesh=mesh, in_specs=in_specs, out_specs=out_specs, check_vma=False
    )
```

```python
import functools
import math

import jax
import jax.numpy as jnp
from jax import lax
from jax.experimental import pallas as pl
from jax.experimental.pallas import tpu as pltpu
from jax.sharding import PartitionSpec as P

STEPS = 50
EPS = 1e-06
MESH = pl.DeviceIdType.MESH
F32, BF16 = jnp.float32, jnp.bfloat16

ORDER = (4, 5, 3, 6, 2, 7, 1, 0)
POS = {slot: pos for pos, slot in enumerate(ORDER)}
NZ, NR = 8, 4
FAR_FIRST = (4, 3, 5, 2, 6, 1, 7)
PARTS = 4


def gelu_and_slope(value):
    cdf = 0.5 * (1.0 + lax.erf(value * (1.0 / math.sqrt(2.0))))
    pdf = jnp.exp(-0.5 * value * value) * (1.0 / math.sqrt(2.0 * math.pi))
    return value * cdf, cdf + value * pdf


def nt(left, right):
    return lax.dot_general(left, right, (((1,), (1,)), ((), ())), preferred_element_type=F32)


def tn(left, right):
    return lax.dot_general(left, right, (((0,), (0,)), ((), ())), preferred_element_type=F32)


def kernel(
    lat, steps, ids, table, gains, win, wout, gin, gout,
    w_in, w_out, lats, xn0, h0, sl0, imgs, xn1, sl1, gh1, geps, gh0, hp, pf, pf2, stg1, rcv1, stg2,
    rcv2, idb, hm, pm, pmsg, prcv, pmsg2, prcv2, acc, turned, cstg, crcv, rstg, rrcv, tstg, tsum, trcv,
    local_sem, w_send, w_recv, ag_send, ag_recv, rs_send, rs_recv, id_send, id_recv, p_send, p_recv, p2_send, p2_recv,
    c_send, c_recv, g_send, g_recv, t_send, t_recv,
):
    tok, width = lat.shape[1], lat.shape[2]
    size = tok // PARTS
    hidden = win.shape[2]
    sec, dp, me = lax.axis_index("sec"), lax.axis_index("dp"), lax.axis_index("tp")
    x, ylo, core = dp // 4, (dp // 2) % 2, dp % 2
    y = sec * 2 + ylo
    other = 1 - sec

    def at_z(distance):
        return {"tp": (me + distance + NZ) % NZ}

    def at_x(distance):
        return {"dp": ((x + distance + NR) % NR) * 4 + ylo * 2 + core}

    def at_y(distance):
        there = (y + distance + NR) % NR
        return {"sec": there // 2, "dp": x * 4 + (there % 2) * 2 + core}

    partner = {"dp": x * 4 + ylo * 2 + (1 - core)}
    across = {"sec": other, "dp": x * 4 + (1 - ylo) * 2 + core}

    def remote(src, dst, send_sem, recv_sem, device):
        return pltpu.make_async_remote_copy(
            src_ref=src, dst_ref=dst, send_sem=send_sem, recv_sem=recv_sem,
            device_id=device, device_id_type=MESH,
        )

    def sent(ref, send_sem):
        remote(ref, ref, send_sem, c_recv.at[0, 0], partner).wait_send()

    here = [
        pltpu.make_async_copy(lat.at[sec], lats.at[pl.ds(POS[0] * tok, tok)], local_sem.at[0]),
        pltpu.make_async_copy(win.at[0], w_in.at[sec], local_sem.at[1]),
        pltpu.make_async_copy(wout.at[0], w_out.at[sec], local_sem.at[2]),
    ]
    for copy in here:
        copy.start()
    idb[0] = jnp.full((8, 128), ids[sec], jnp.int32)

    peers = [at(k) for at in (at_z, at_x, at_y) for k in (1, -1)] + [partner]
    barrier = pltpu.get_barrier_semaphore()
    for peer in peers:
        pl.semaphore_signal(barrier, inc=1, device_id=peer, device_id_type=MESH)
    pl.semaphore_wait(barrier, len(peers))

    def far(part, way):
        return part // (PARTS // 2) == way

    far_parts = [(p + way * (PARTS // 2), way) for p in range(PARTS // 2) for way in (0, 1)]
    near_parts = [(p + (1 - way) * (PARTS // 2), way) for p in range(PARTS // 2) for way in (0, 1)]

    def gather_copy(buf, way, step, part):
        if way == 0:
            src, dst, device = POS[step - 1], POS[step], at_z(1)
        else:
            src, dst, device = POS[(NZ - step + 1) % NZ], POS[NZ - step], at_z(-1)
        at = (way, PARTS * (step - 1) + part)
        return remote(
            buf.at[pl.ds(src * tok + part * size, size)],
            buf.at[pl.ds(dst * tok + part * size, size)],
            ag_send, ag_recv.at[at], device,
        )

    def gather_begin(buf, parts):
        for part, way in parts:
            gather_copy(buf, way, 1, part).start()

    def gather_parts(buf, step, parts):
        for part, way in parts:
            gather_copy(buf, way, step, part).wait_recv()
            if step + 1 < NZ // 2 or (step + 1 == NZ // 2 and far(part, way)):
                gather_copy(buf, way, step + 1, part).start()

    def gather_step(buf, step):
        gather_parts(buf, step, far_parts)
        if step < NZ // 2:
            gather_parts(buf, step, near_parts)

    def gather_with(buf, work, middle=None):
        work(*arrived(0))
        gather_step(buf, 1)
        for step in (1, 2):
            start, count = arrived(step)
            work(start, tok)
            gather_parts(buf, step + 1, far_parts)
            work(start + tok, tok)
            if step == 2 and middle is not None:
                middle()
            gather_parts(buf, step + 1, near_parts)
        work(*arrived(3))

    def arrived(step):
        if step == 0:
            return POS[0] * tok, tok
        if step == NZ // 2:
            return 0, tok
        return POS[NZ - step] * tok, 2 * tok

    def scatter_copy(stg, rcv, way, step, part):
        at = (way, PARTS * (step - 1) + part)
        rows = pl.ds(part * size, size)
        return remote(
            stg.at[way, step - 1, rows], rcv.at[way, step - 1, rows],
            rs_send, rs_recv.at[at], at_z(1) if way == 0 else at_z(-1),
        )

    def scatter_step(stg, rcv, step):
        for part, way in (near_parts if step > 1 else []) + far_parts:
            at = pl.ds(part * size, size)
            base = part * size + (way * tok if step > 1 else 0)
            value = pf[pl.ds(base, size), :]
            if step > 2 or (step == 2 and far(part, way)):
                scatter_copy(stg, rcv, way, step - 1, part).wait_recv()
                value = value + rcv[way, step - 2, at, :].astype(F32)
            stg[way, step - 1, at, :] = value.astype(BF16)
            scatter_copy(stg, rcv, way, step, part).start()

    def scatter_end(stg, rcv, part):
        for way in (0, 1):
            scatter_copy(stg, rcv, way, NZ // 2, part).wait_recv()

    def chunk(step):
        return arrived(5 - step) if step > 1 else (0, tok)

    quarter = (x + 2 * ylo) % NR

    def piece(offset, which, h):
        rows = (quarter + offset) % NR * (width // NR) + which * (width // NR // 2)
        return pl.ds(pl.multiple_of(rows + h * (width // NR // 4), 16), width // NR // 4)

    held = (w_in, w_out)
    given = (win, wout)
    beside = {"dp": x * 4 + (1 - ylo) * 2 + core}

    def weight_copy(a, kind, h):
        if kind == 0:
            rows = piece(2, core, h)
            src, dst, device = given[a].at[0, rows], held[a].at[sec, rows], across
        else:
            rows = piece((0, 0, 0, 0, 0, 3, 1, 2)[kind], core, h)
            src = dst = held[a].at[other, rows]
            device = (at_x(1), at_x(-1), beside, partner)[min(kind, 4) - 1]
        return remote(src, dst, w_send, w_recv.at[a, kind, h], device)

    def weight_landed(a, kind, h):
        ref = held[a].at[other, piece((0, 3, 1, 2)[kind % 4], core if kind < 4 else 1 - core, h)]
        remote(ref, ref, w_send, w_recv.at[a, kind, h], partner).wait_recv()

    def weights_first(a, h):
        weight_landed(a, 0, h)
        for kind in (1, 2, 3, 4):
            weight_copy(a, kind, h).start()

    def weights_second(a, h):
        for kind in (1, 2, 3):
            weight_landed(a, kind, h)
            weight_copy(a, kind + 4, h).start()

    def weights_last(a):
        for h in (0, 1):
            for kind in (4, 5, 6, 7):
                weight_landed(a, kind, h)

    def each(count, rows, body, init=None):
        several = min(4, count // rows)

        def group(i, carry):
            for j in range(several):
                carry = body(pl.multiple_of((i * several + j) * rows, rows), carry)
            return carry

        return lax.fori_loop(0, count // rows // several, group, init)

    def norm(buf, dst, start, count, gain, slots=None):
        def body(at, total):
            value = buf[pl.ds(start + at, 16), :].astype(F32)
            scale = lax.rsqrt(jnp.mean(value * value, axis=-1, keepdims=True) + EPS)
            dst[pl.ds(start + at, 16), :] = (value * scale * gain).astype(BF16)
            return None if total is None else total + value[:8] + value[8:]

        if slots is None:
            each(count, 16, body)
            return
        for index, slot in enumerate(slots):
            start = POS[slot] * tok
            total = each(tok, 16, body, jnp.zeros((8, width), F32))
            pm[pl.ds(slot, 1), :] = jnp.sum(total, axis=0, keepdims=True) * (1.0 / tok)

    def slots_of(start, count):
        return ORDER[start // tok:(start + count) // tok]

    theta = (jnp.full((1, 128), steps[sec], jnp.int32).astype(F32) + 1.0) * (
        math.pi / 2.0 / (STEPS + 1.0)
    )
    alpha, sigma = jnp.cos(theta)[:, :1], jnp.sin(theta)[:, :1]
    for a in (0, 1):
        for h in (0, 1):
            weight_copy(a, 0, h).start()
    here[0].wait()
    gather_begin(lats, far_parts + near_parts)
    gain0, gain1 = gains[0:1, :], gains[1:2, :]
    norm(lats, xn0, *arrived(0), gain0)
    gather_step(lats, 1)
    weights_first(0, 0)
    norm(lats, xn0, *arrived(1), gain0)
    weights_first(0, 1)
    gather_step(lats, 2)
    weights_first(1, 0)
    weights_second(0, 0)
    norm(lats, xn0, *arrived(2), gain0)
    weights_first(1, 1)
    weights_second(0, 1)
    gather_step(lats, 3)
    weights_second(1, 0)
    norm(lats, xn0, *arrived(3), gain0)
    gather_step(lats, 4)
    weights_second(1, 1)
    for k in range(1, NZ):
        remote(idb.at[0], idb.at[k], id_send, id_recv.at[k - 1], at_z(k)).start()
    norm(lats, xn0, *arrived(4), gain0)
    here[1].wait()
    weights_last(0)

    def hidden0(start, count):
        hp[pl.ds(0, count), :] = jnp.dot(
            xn0[pl.ds(start, count), :], w_in[0], preferred_element_type=F32
        )

        def body(at, carry):
            act, slope = gelu_and_slope(hp[pl.ds(at, 16), :])
            h0[pl.ds(start + at, 16), :] = act.astype(BF16)
            sl0[pl.ds(start + at, 16), :] = slope
            return carry

        each(count, 16, body)

    hidden0(*chunk(1))
    here[2].wait()
    weights_last(1)

    for step in range(1, 6):
        start, count = chunk(step)
        if step > 1:
            hidden0(start, count)
        out = nt(h0[pl.ds(start, count), :], w_out[0])
        if step < 5:
            pf[pl.ds(0, count), :] = out
            scatter_step(stg1, rcv1, step)
        else:
            pf2[...] = out

    own = POS[0] * tok
    sent(lats.at[pl.ds(0, (NZ - 1) * tok)], ag_send)
    for part, way in far_parts:
        scatter_end(stg1, rcv1, part)

        def images(at, carry):
            rows = pl.ds(part * size + at, 16)
            base = lats[pl.ds(own + part * size + at, 16), :].astype(F32)
            mix = pf2[rows, :] + (rcv1[0, 3, rows, :].astype(F32) + rcv1[1, 3, rows, :].astype(F32))
            imgs[pl.ds(own + part * size + at, 16), :] = (
                (base - sigma * (base + mix)) / alpha
            ).astype(BF16)
            return carry

        each(size, 16, images)
        gather_begin(imgs, [(part, way)])

    gather_begin(imgs, near_parts)

    def hidden1(start, count):
        slots = slots_of(start, count)
        norm(imgs, xn1, start, count, gain1, slots)
        hp[pl.ds(0, count), :] = jnp.dot(
            xn1[pl.ds(start, count), :], w_in[1], preferred_element_type=F32
        )
        for index, slot in enumerate(slots):
            def body(at, total):
                act, slope = gelu_and_slope(hp[pl.ds(index * tok + at, 16), :])
                sl1[pl.ds(start + index * tok + at, 16), :] = slope
                act = act.astype(BF16).astype(F32)
                return total + act[:8] + act[8:]

            total = each(tok, 16, body, jnp.zeros((8, hidden), F32))
            hm[pl.ds(slot, 1), :] = jnp.sum(total, axis=0, keepdims=True) * (1.0 / tok)

    for k in range(1, NZ):
        remote(idb.at[k], idb.at[k], id_send, id_recv.at[k - 1], at_z(k)).wait_recv()
    id_rows = jnp.concatenate([idb[k, 0:1, :] for k in range(NZ)], axis=0)
    prompts = table.shape[0]
    onehot = (
        id_rows[:, :prompts] == lax.broadcasted_iota(jnp.int32, (NZ, prompts), 1)
    ).astype(F32).astype(BF16)
    text = jnp.dot(onehot, table[...], preferred_element_type=F32)
    text = text * lax.rsqrt(jnp.mean(text * text, axis=-1, keepdims=True) + EPS)
    def mixed_rows(rows):
        high = rows.astype(BF16).astype(F32)
        both = jnp.concatenate([high, rows - high], axis=0).astype(BF16)
        out = nt(both, w_out[1])
        return out[:NZ] + out[NZ:]

    def exchange(message, arrivals, send_sem, recv_sem, k):
        return remote(message, arrivals.at[k - 1], send_sem, recv_sem.at[k - 1], at_z(k))

    mid = width // 2
    opposite = NZ // 2
    hm[pl.ds(opposite, 1), :] = jnp.zeros((1, hidden), F32)
    gather_with(imgs, hidden1)
    mixed = mixed_rows(hm[...])
    pmsg[...] = jnp.concatenate([mixed[:, :mid], mixed[:, mid:]], axis=0).astype(BF16)
    for k in FAR_FIRST:
        exchange(pmsg, prcv, p_send, p_recv, k).start()
    gather_parts(imgs, 4, far_parts)
    hidden1(*arrived(4))

    lanes = width // 128
    last = mixed_rows(jnp.broadcast_to(hm[pl.ds(opposite, 1), :], (NZ, hidden)))[0:1]
    pmsg2[...] = jnp.concatenate(
        [last[:, 128 * i:128 * i + 128] for i in range(lanes)] + [jnp.zeros((16 - lanes, 128), F32)],
        axis=0,
    ).astype(BF16)
    for k in FAR_FIRST:
        exchange(pmsg2, prcv2, p2_send, p2_recv, k).start()
    pooled = pm[...] + mixed
    for k in range(1, NZ):
        exchange(pmsg, prcv, p_send, p_recv, k).wait_recv()
        got = prcv[k - 1].astype(F32)
        got = jnp.concatenate([got[:NZ], got[NZ:]], axis=1)
        pooled = pooled + jnp.concatenate([got[NZ - k:], got[:NZ - k]], axis=0)
    rows = {opposite: last}
    for k in range(1, NZ):
        exchange(pmsg2, prcv2, p2_send, p2_recv, k).wait_recv()
        got = prcv2[k - 1].astype(F32)
        rows[(opposite + k) % NZ] = jnp.concatenate([got[i:i + 1] for i in range(lanes)], axis=1)
    pooled = pooled + jnp.concatenate([rows[k] for k in range(NZ)], axis=0)
    unit = lax.rsqrt(jnp.mean(pooled * pooled, axis=-1, keepdims=True) + EPS)
    g_mean = (unit * text - pooled * (unit * unit * unit) * jnp.mean(
        pooled * text, axis=-1, keepdims=True
    )) * (-100.0 / width / tok)
    g_h1 = jnp.dot(g_mean.astype(BF16), w_out[1], preferred_element_type=F32)
    g_own = g_mean[0:1, :]
    sent(lats.at[pl.ds(0, (NZ - 1) * tok)], rs_send)

    for step in range(1, 6):
        start, count = chunk(step)
        for index, slot in enumerate(slots_of(start, count)):
            row = g_h1[slot:slot + 1, :]

            def slope_times(at, carry):
                rows = pl.ds(start + index * tok + at, 16)
                gh1[rows, :] = (row * sl1[rows, :]).astype(BF16)
                return carry

            each(tok, 16, slope_times)
        out = nt(gh1[pl.ds(start, count), :], w_in[1])
        if step < 5:
            pf[pl.ds(0, count), :] = out
            scatter_step(stg2, rcv2, step)
        else:
            pf2[...] = out

    ratio = -(sigma / alpha)
    sent(lats.at[pl.ds(0, (NZ - 1) * tok)], ag_send)
    seen_own = imgs[pl.ds(own, tok), :].astype(F32)
    scales = lax.rsqrt(jnp.mean(seen_own * seen_own, axis=-1, keepdims=True) + EPS)
    for part, way in far_parts:
        scatter_end(stg2, rcv2, part)

        def back(at, carry):
            rows = pl.ds(part * size + at, 16)
            seen = imgs[pl.ds(own + part * size + at, 16), :].astype(F32)
            g_xn = pf2[rows, :] + (
                rcv2[0, 3, rows, :].astype(F32) + rcv2[1, 3, rows, :].astype(F32)
            )
            scale = scales[part * size:part * size + size]
            weighted = gain1 * g_xn
            g_norm = scale * weighted - seen * (scale * scale * scale) * jnp.mean(
                seen * weighted, axis=-1, keepdims=True
            )
            g_images = (g_own + g_norm).astype(BF16).astype(F32)
            geps[pl.ds(own + part * size + at, 16), :] = (ratio * g_images).astype(BF16)
            return carry

        each(size, 16, back)
        gather_begin(geps, [(part, way)])

    gather_begin(geps, near_parts)

    def hidden_back(start, count):
        hp[pl.ds(0, count), :] = jnp.dot(
            geps[pl.ds(start, count), :], w_out[0], preferred_element_type=F32
        )

        def body(at, carry):
            rows = pl.ds(start + at, 16)
            gh0[rows, :] = (hp[pl.ds(at, 16), :] * sl0[rows, :]).astype(BF16)
            return carry

        each(count, 16, body)

    def weight_terms(a, start, count):
        left, right = ((geps, h0), (xn0, gh0))[a]
        rows = pl.ds(start, count)

        for i in range(width // 256):
            cols = pl.ds(i * 256, 256)
            acc[a, cols, :] = tn(left[rows, cols], right[rows, :])

    def rows_of(a, slab, j, which):
        cx, cy = (slab, j) if a == 0 else (j, slab)
        return pl.ds(pl.multiple_of((cy // 2) * 640 + cx * 160 + (cy % 2) * 80 + which * 40, 40), 40)

    def pair(a, slab, part, which):
        return jnp.concatenate(
            [acc[a, rows_of(a, slab, 2 * part + j, which), :] for j in (0, 1)], axis=0
        )

    place = (x, y)
    along = (at_x, at_y)

    def core_copy(a, n):
        slab = (place[a] + (2, 1, 3, 0)[n]) % NR
        return remote(cstg.at[a, slab], crcv.at[a, slab], c_send, c_recv.at[a, n], partner)

    def early_terms():
        weight_terms(0, 4 * tok, 4 * tok)
        weight_terms(1, 4 * tok, 4 * tok)

    def slab_terms(a, n):
        slab = (place[a] + (2, 1, 3, 0)[n]) % NR
        if a == 0:
            blocks = [(s * 640 + slab * 160, 160) for s in (0, 1)]
        else:
            blocks = [((slab // 2) * 640 + cx * 160 + (slab % 2) * 80, 80) for cx in range(NR)]
        right = (h0, gh0)[a][pl.ds(0, 4 * tok), :]
        for start, count in blocks:
            rows = pl.ds(pl.multiple_of(start, 16), count)
            acc[a, rows, :] += jnp.dot(turned[a, rows, :], right, preferred_element_type=F32)
        for part in (0, 1):
            cstg[a, slab, pl.ds(80 * part, 80), :] = pair(a, slab, part, 1 - core).astype(BF16)
        core_copy(a, n).start()

    turned[1] = xn0[pl.ds(0, 4 * tok), :].T
    gather_with(geps, hidden_back, early_terms)
    gather_parts(geps, 4, far_parts)
    turned[0] = geps[pl.ds(0, 4 * tok), :].T
    slab_terms(0, 0)
    hidden_back(*arrived(4))
    for a, n in ((1, 0), (0, 1), (1, 1), (0, 2), (1, 2)):
        slab_terms(a, n)

    def own_part(a, distance, part):
        slab = (place[a] + distance) % NR
        return pair(a, slab, part, core) + crcv[a, slab, pl.ds(80 * part, 80), :].astype(F32)

    def ring_copy(a, way, step, part):
        at = (a, way, 2 * (step - 1) + part)
        rows = pl.ds(80 * part, 80)
        return remote(
            rstg.at[a, way, step - 1, rows], rrcv.at[a, way, step - 1, rows],
            g_send, g_recv.at[at], along[a](1 if way == 0 else -1),
        )

    def ring_send(a, way, step, part):
        distance = 2 if step == 1 else (1 if way == 0 else 3)
        value = own_part(a, distance, part)
        if step == 2 and part == way:
            ring_copy(a, way, 1, part).wait_recv()
            value = value + rrcv[a, way, 0, pl.ds(80 * part, 80), :].astype(F32)
        rstg[a, way, step - 1, pl.ds(80 * part, 80), :] = value.astype(BF16)
        ring_copy(a, way, step, part).start()

    for a in (0, 1):
        core_copy(a, 0).wait_recv()
        for way in (0, 1):
            ring_send(a, way, 1, way)
    for way in (0, 1):
        for a in (0, 1):
            core_copy(a, 1 + way).wait_recv()
            ring_send(a, way, 2, 1 - way)
    for a in (0, 1):
        slab_terms(a, 3)
    for a in (0, 1):
        for way in (0, 1):
            ring_send(a, way, 2, way)

    def last_copy(a, k):
        target = (place[1 - a] + k) % NR
        return remote(
            tstg.at[a, target], trcv.at[a, k - 1], t_send, t_recv.at[a, k - 1],
            along[1 - a](k),
        )

    for a in (0, 1):
        core_copy(a, 3).wait_recv()
        for part in (0, 1):
            value = own_part(a, 0, part)
            for way in (0, 1):
                ring_copy(a, way, 2, part).wait_recv()
                value = value + rrcv[a, way, 1, pl.ds(80 * part, 80), :].astype(F32)
            for j in (0, 1):
                rows = value[40 * j:40 * j + 40]
                tsum[a, 2 * part + j] = rows
                tstg[a, 2 * part + j] = jnp.concatenate(
                    [rows, jnp.zeros((8, hidden), F32)], axis=0
                ).astype(BF16)
        for k in (2, 1, 3):
            last_copy(a, k).start()
    for a, result in enumerate((gout, gin)):
        total = tsum[a, place[1 - a]]
        for k in range(1, NR):
            last_copy(a, k).wait_recv()
            total = total + trcv[a, k - 1].astype(F32)[:40]
        result[...] = total
    sent(lats.at[pl.ds(0, (NZ - 1) * tok)], ag_send)
    sent(lats.at[pl.ds(0, (NZ - 1) * tok)], rs_send)
    sent(w_in, w_send)
    sent(idb.at[pl.ds(0, NZ - 1)], id_send)
    sent(prcv, p_send)
    sent(prcv2, p2_send)
    sent(crcv, c_send)
    sent(w_in.at[0, pl.ds(0, 960)], g_send)
    sent(trcv, t_send)


def hand_over(left, right, left_out, right_out):
    left_out[...] = left[...]
    right_out[...] = right[...]


def on_device(latents, timesteps, prompt_ids, prompt_table, gains, w_in, w_out):
    tok, width = latents.shape[1:]
    hidden = w_in.shape[2]
    rows = NZ * tok
    vmem, dma = pltpu.VMEM, pltpu.SemaphoreType.DMA
    scratch = [
        vmem((2, width, hidden), BF16),
        vmem((2, width, hidden), BF16),
        vmem((rows, width), BF16),
        vmem((rows, width), BF16),
        vmem((rows, hidden), BF16),
        vmem((rows, hidden), F32),
        vmem((rows, width), BF16),
        vmem((rows, width), BF16),
        vmem((rows, hidden), F32),
        vmem((rows, hidden), BF16),
        vmem((rows, width), BF16),
        vmem((rows, hidden), BF16),
        vmem((2 * tok, hidden), F32),
        vmem((2 * tok, width), F32),
        vmem((tok, width), F32),
        vmem((2, 4, tok, width), BF16),
        vmem((2, 4, tok, width), BF16),
        vmem((2, 4, tok, width), BF16),
        vmem((2, 4, tok, width), BF16),
        vmem((NZ, 8, 128), jnp.int32),
        vmem((NZ, hidden), F32),
        vmem((NZ, width), F32),
        vmem((2 * NZ, width // 2), BF16),
        vmem((NZ - 1, 2 * NZ, width // 2), BF16),
        vmem((16, 128), BF16),
        vmem((NZ - 1, 16, 128), BF16),
        vmem((2, width, hidden), F32),
        vmem((2, width, rows // 2), BF16),
        vmem((2, NR, 160, hidden), BF16),
        vmem((2, NR, 160, hidden), BF16),
        vmem((2, 2, 2, 160, hidden), BF16),
        vmem((2, 2, 2, 160, hidden), BF16),
        vmem((2, NR, 48, hidden), BF16),
        vmem((2, NR, 40, hidden), F32),
        vmem((2, NR - 1, 48, hidden), BF16),
        dma((3,)),
        dma(()), dma((2, 8, 2)),
        dma(()), dma((2, 4 * PARTS)),
        dma(()), dma((2, 4 * PARTS)),
        dma(()), dma((7,)),
        dma(()), dma((7,)),
        dma(()), dma((7,)),
        dma(()), dma((2, 4)),
        dma(()), dma((2, 2, 4)),
        dma(()), dma((2, 3)),
    ]
    whole, scalar, away = (pl.BlockSpec(memory_space=s) for s in (pltpu.VMEM, pltpu.SMEM, pl.ANY))
    share = jax.ShapeDtypeStruct((width // 32, hidden), F32)
    shares = pl.pallas_call(
        kernel,
        out_shape=(share, share),
        in_specs=[away, scalar, scalar, whole, whole, away, away],
        out_specs=(whole, whole),
        scratch_shapes=scratch,
        compiler_params=pltpu.CompilerParams(
            collective_id=0, has_side_effects=True, vmem_limit_bytes=56 * 2**20
        ),
        name="draft_step",
    )(latents, timesteps, prompt_ids, prompt_table, gains, w_in, w_out)
    return pl.pallas_call(hand_over, out_shape=(share, share), name="hand_over")(*shares)


def solution(mesh):
    in_specs = (
        P(("dp", "tp"), None, None),
        P(("dp", "tp")),
        P(("dp", "tp")),
        P(),
        P(),
        P("sec", None, "tp"),
        P("sec", None, "tp"),
    )
    out_specs = (P(("sec", "dp"), "tp"), P(("sec", "dp"), "tp"))
    return jax.shard_map(
        on_device, mesh=mesh, in_specs=in_specs, out_specs=out_specs, check_vma=False
    )
```
